128 devices in a mesh: dp: 16 (over z, x_hi, core), context: 2 (over x_lo), tensor: 4 (over y).
Axes of the slice: x: 4 (x_hi: 2, x_lo: 2; x = x_hi * 2 + x_lo), y: 4, z: 4, core: 2. Of those that a mesh axis runs over, the one named last changes fastest.
Arguments:
- hidden: bfloat16 [32768, 5120], P(('dp', 'context'), 'tensor'), may hold values from -4 to 4
- seq_id: int32 [32768], P(('dp', 'context')), may hold values from 0 to 511, as said below
- dest_page: int32 [512], P(('dp', 'context')), may hold values from 0 to 255, as said below
- norm_gain: bfloat16 [5120], replicated, may hold values from 0.099609375 to 1.8984375
- w_query: bfloat16 [5120, 2560], P(None, 'tensor'), may hold values from -0.078125 to 0.078125
- q_bias: bfloat16 [2560], P('tensor'), may hold values from -120 to 120
- w_key: bfloat16 [5120, 512], P(None, 'tensor'), may hold values from -0.078125 to 0.078125
- w_value: bfloat16 [5120, 512], P(None, 'tensor'), may hold values from -0.078125 to 0.078125
- v_bias: bfloat16 [512], P('tensor'), may hold values from -3 to 3
- w_out: bfloat16 [2560, 5120], P('tensor'), may hold values from -0.125 to 0.125
Outputs:
- mixed: bfloat16 [32768, 5120], P(('dp', 'context'), 'tensor')
The draws below stay inside these ranges and needn't reach their ends.
Inputs may be any that keep to these rules, and one draw needn't show every extreme that they name: `dest_page`: for each context index the values of all owners' pages form a permutation; page p of owner o on context index c is assigned to group value // 16, page value % 16 of that group's device with the same context index; the two context indices of an owner send their page p to the same group; at most 1 pages of one owner device go to one group, and some owner device sends exactly 1. `seq_id`: all tokens of a page share a value; a value is held only by pages assigned to one group.
All inputs are finite; a program needn't handle non-finite values.
Results may differ from the reference program's by a relative error of at most 0.018.
Values may be sent and summed in bfloat16 or wider, within the bound.
No kernel may reach another device: no remote copies, remote signals or barrier semaphores. Data moves between devices by JAX's collectives and lax.ppermute only.
A program may use at most 192 MiB of HBM per device.

```python
import math
import jax
import jax.numpy as jnp
from jax import lax

D = 5120
HEADS = 20
KV_HEADS = 4
HEAD = 128
PAGE = 64
PAGES_DEV = 16
TOK_DEV = 1024
TOKENS = 32768
N_DP = 16
N_CONTEXT = 2


def page_targets(key):
    first = jax.random.fold_in(key, 11)
    second = jax.random.fold_in(key, 12)
    shifts = jax.random.permutation(first, N_DP).astype(jnp.int32)
    places = jax.random.permutation(second, PAGES_DEV).astype(jnp.int32)
    entry = jnp.arange(N_DP * N_CONTEXT * PAGES_DEV, dtype=jnp.int32)
    owner = entry // (N_CONTEXT * PAGES_DEV)
    page = entry % PAGES_DEV
    group = (owner + shifts[page % N_DP]) % N_DP
    return (group * PAGES_DEV + places[page]).astype(jnp.int32)


def draw_dest_page(key, part):
    targets = page_targets(key)
    return targets


def draw_seq_id(key, part):
    targets = page_targets(key)
    key = jax.random.fold_in(key, 2)
    columns_all = N_CONTEXT * PAGES_DEV
    starts = jax.random.randint(key, (N_DP, columns_all), 0, 12) == 0
    column = jnp.arange(columns_all, dtype=jnp.int32)
    starts = jnp.where(column[None, :] == 0, True, starts)
    starts = jnp.where(column[None, :] == PAGES_DEV // 2, True, starts)
    runs = jnp.cumsum(starts.astype(jnp.int32), axis=1) - 1
    last_run = runs[:, -1:]
    runs = jnp.where(runs == last_run, columns_all - 1, runs).astype(jnp.int32)
    token = jnp.arange(TOKENS, dtype=jnp.int32)
    device = token // TOK_DEV
    page = device * PAGES_DEV + token % TOK_DEV // PAGE
    target = targets[page]
    group = target // PAGES_DEV
    column_of = device % N_CONTEXT * PAGES_DEV + target % PAGES_DEV
    return (group * columns_all + runs[group, column_of]).astype(jnp.int32)


def draw_q_bias(key, part):
    key = jax.random.fold_in(key, 3)
    base = jnp.clip(jax.random.normal(key, (HEADS, HEAD), jnp.float32), -3.0, 3.0)
    values = base * 0.5
    return values.reshape(HEADS * HEAD).astype(jnp.bfloat16)


def block_levels(stream_key, shape, shards, smallest, largest):
    def one(position, shards_of):
        steps = jax.random.uniform(jax.random.fold_in(jax.random.fold_in(stream_key, 6), position), (shards_of,), jnp.float32, smallest / len(shards), largest / len(shards))
        return jnp.repeat(jnp.exp(steps), shape[position] // shards_of).reshape((-1,) + (1,) * (len(shape) - position - 1))

    loudness = one(*shards[0])
    for cut in shards[1:]:
        loudness = loudness * one(*cut)
    return loudness


def centred(stream_key, dims, spread, reach, pieces=(), kind=jnp.bfloat16):
    loudness = block_levels(stream_key, dims, pieces, -0.22, 0.18) if pieces else 1.0
    values = jax.random.normal(stream_key, dims, jnp.float32) * spread * loudness
    return jnp.minimum(jnp.maximum(values, -reach), reach).astype(kind)


def setup_inputs(seed: int = 0) -> dict:
    key_list = jax.random.split(jax.random.key(seed), 11)
    hidden = centred(key_list[0], (TOKENS, D), 0.5, 4.0, ((0, 32), (1, 4)))
    seq_id = draw_seq_id(jax.random.fold_in(key_list[10], 71), 0)
    dest_page = draw_dest_page(jax.random.fold_in(key_list[10], 71), 0)
    norm_gain = jnp.clip(1.0 + 0.18 * jax.random.normal(key_list[3], (D,), jnp.float32), 0.099609375, 1.8984375).astype(jnp.bfloat16)
    w_query = centred(key_list[4], (D, HEADS * HEAD), D ** -0.5, 0.078125, ((1, 4),))
    q_bias = draw_q_bias(jax.random.fold_in(key_list[10], 71), 0)
    w_key = centred(key_list[6], (D, KV_HEADS * HEAD), D ** -0.5, 0.078125, ((1, 4),))
    w_value = centred(key_list[7], (D, KV_HEADS * HEAD), D ** -0.5, 0.078125, ((1, 4),))
    v_bias = centred(key_list[8], (KV_HEADS * HEAD,), 0.5, 3.0, ((0, 4),))
    w_out = centred(key_list[9], (HEADS * HEAD, D), (HEADS * HEAD) ** -0.5, 0.125, ((0, 4),))
    return dict(hidden=hidden, seq_id=seq_id, dest_page=dest_page, norm_gain=norm_gain, w_query=w_query, q_bias=q_bias, w_key=w_key, w_value=w_value, v_bias=v_bias, w_out=w_out)


EPSILON = 1e-06

def reference(hidden, seq_id, dest_page, norm_gain, w_query, q_bias, w_key, w_value, v_bias, w_out):
    wide = hidden.astype(jnp.float32)
    scale = lax.rsqrt(lax.optimization_barrier(jnp.mean(wide * wide, axis=1, keepdims=True)) + EPSILON)
    normed = (wide * scale * norm_gain.astype(jnp.float32)).astype(jnp.bfloat16)
    queries = (jnp.dot(normed, w_query, preferred_element_type=jnp.float32) + q_bias.astype(jnp.float32)).astype(jnp.bfloat16)
    key_rows = jnp.dot(normed, w_key, preferred_element_type=jnp.float32).astype(jnp.bfloat16)
    value_rows = (jnp.dot(normed, w_value, preferred_element_type=jnp.float32) + v_bias.astype(jnp.float32)).astype(jnp.bfloat16)
    token = jnp.arange(TOKENS, dtype=jnp.int32)
    device = token // TOK_DEV
    context = device % N_CONTEXT
    page = device * PAGES_DEV + token % TOK_DEV // PAGE
    target = dest_page[page]
    group = target // PAGES_DEV
    place = context * TOK_DEV + target % PAGES_DEV * PAGE + token % PAGE
    layout = (group * (N_CONTEXT * TOK_DEV) + place).astype(jnp.int32)
    span = N_CONTEXT * TOK_DEV
    members = HEADS // KV_HEADS

    def arrange(values):
        return jnp.zeros_like(values).at[layout].set(values)
    grouped_q = arrange(queries).reshape(N_DP, span, KV_HEADS, members, HEAD)
    grouped_k = arrange(key_rows).reshape(N_DP, span, KV_HEADS, HEAD)
    grouped_v = arrange(value_rows).reshape(N_DP, span, KV_HEADS, HEAD)
    grouped_s = arrange(seq_id).reshape(N_DP, span)
    order = jnp.arange(span, dtype=jnp.int32)

    def one_group(inputs):
        group_q, group_k, group_v, group_s = inputs
        scores = jnp.einsum('tkgd,rkd->kgtr', group_q.astype(jnp.float32), group_k.astype(jnp.float32), precision=lax.Precision.HIGHEST) / math.sqrt(HEAD)
        visible = (group_s[:, None] == group_s[None, :]) & (order[None, :] <= order[:, None])
        scores = jnp.where(visible, scores, -1e+30)
        highest = lax.optimization_barrier(jnp.max(scores, axis=3, keepdims=True))
        weight = jnp.where(visible, jnp.exp(scores - highest), 0.0)
        total = lax.optimization_barrier(jnp.sum(weight, axis=3))
        rounded = lax.optimization_barrier(weight.astype(jnp.bfloat16))
        summed = jnp.einsum('kgtr,rkd->tkgd', rounded.astype(jnp.float32), group_v.astype(jnp.float32), precision=lax.Precision.HIGHEST)
        result = summed / jnp.transpose(total, (2, 0, 1))[..., None]
        return result.reshape(span, HEADS * HEAD).astype(jnp.bfloat16)
    attention = lax.map(one_group, (grouped_q, grouped_k, grouped_v, grouped_s))
    attention = attention.reshape(TOKENS, HEADS * HEAD)[layout]
    projected = jnp.dot(attention, w_out, preferred_element_type=jnp.float32)
    return (wide + projected).astype(jnp.bfloat16)
```

```python
import math

import jax
import jax.numpy as jnp
from jax import lax
from jax.experimental import pallas as pl
from jax.experimental.pallas import tpu as pltpu
from jax.sharding import Mesh
from jax.sharding import PartitionSpec as P

HEAD = 128
PAGE = 64
EPSILON = 1e-06
DP = ("z", "xh", "core")
TENSOR = 4
STEP = 16
VMEM_BYTES = 60 * 1024 * 1024


def ring_gather(block):
    right = [(i, (i + 1) % TENSOR) for i in range(TENSOR)]
    left = [(i, (i - 1) % TENSOR) for i in range(TENSOR)]
    half = block.shape[0] // 2
    from_left = lax.ppermute(block, "tensor", right)
    from_right = lax.ppermute(block, "tensor", left)
    far_top = lax.ppermute(from_left[:half], "tensor", right)
    far_low = lax.ppermute(from_right[half:], "tensor", left)
    return (block, from_left, from_right, far_top, far_low)


def project_kernel(
    order, group, own, left, right, far_top, far_low, gain, w_query, w_key, w_value, q_bias, v_bias,
    out, total, squares,
):
    step = pl.program_id(0)
    rows, width = own.shape

    def add(piece, start, count):
        wide = piece[...].astype(jnp.float32)
        square = jnp.sum(wide * wide, axis=1, keepdims=True)
        scaled = (wide * gain[0].astype(jnp.float32)).astype(jnp.bfloat16)
        products = jnp.concatenate(
            [
                jnp.dot(scaled, w[...], preferred_element_type=jnp.float32)
                for w in (w_query, w_key, w_value)
            ],
            axis=1,
        )
        at = pl.ds(start, count)
        return at, square, products

    @pl.when(step == 0)
    def _():
        at, square, products = add(own, 0, rows)
        total[at], squares[at] = products, square

    for index, pieces in ((1, (left,)), (2, (right,)), (3, (far_top, far_low))):

        @pl.when(step == index)
        def _(pieces=pieces):
            start = 0
            for piece in pieces:
                at, square, products = add(piece, start, piece.shape[0])
                total[at] = total[at] + products
                squares[at] = squares[at] + square
                start += piece.shape[0]

    @pl.when(step == 3)
    def _():
        scale = lax.rsqrt(squares[...] * (1.0 / (TENSOR * width)) + EPSILON)
        queries = w_query.shape[1]
        keys = queries + w_key.shape[1]
        result = total[...] * scale
        result = jnp.concatenate(
            [
                result[:, :queries] + q_bias[...].astype(jnp.float32),
                result[:, queries:keys],
                result[:, keys:] + v_bias[...].astype(jnp.float32),
            ],
            axis=1,
        ).astype(jnp.bfloat16)
        count = out.shape[1]
        for page in range(out.shape[0]):
            out[group[page]] = result[page * count : (page + 1) * count]


def project(order, group, pieces, gain, w_query, w_key, w_value, q_bias, v_bias):
    rows, width = pieces[0].shape
    pages = group.shape[0]
    columns = w_query.shape[1] + w_key.shape[1] + w_value.shape[1]

    def whole(a):
        return pl.BlockSpec(a.shape, lambda k, order, group: (0,) * a.ndim)

    def band(w):
        return pl.BlockSpec((width, w.shape[1]), lambda k, order, group: (order[k], 0))

    gain = gain.reshape(TENSOR, 1, width)
    q_bias, v_bias = q_bias[None, :], v_bias[None, :]
    return pl.pallas_call(
        project_kernel,
        out_shape=jax.ShapeDtypeStruct((pages, rows // pages, columns), jnp.bfloat16),
        grid_spec=pltpu.PrefetchScalarGridSpec(
            num_scalar_prefetch=2,
            grid=(TENSOR,),
            in_specs=[whole(p) for p in pieces]
            + [
                pl.BlockSpec((1, 1, width), lambda k, order, group: (order[k], 0, 0)),
                band(w_query),
                band(w_key),
                band(w_value),
                whole(q_bias),
                whole(v_bias),
            ],
            out_specs=pl.BlockSpec(
                (pages, rows // pages, columns), lambda k, order, group: (0, 0, 0)
            ),
            scratch_shapes=[
                pltpu.VMEM((rows, columns), jnp.float32),
                pltpu.VMEM((rows, 1), jnp.float32),
            ],
        ),
        compiler_params=pltpu.CompilerParams(vmem_limit_bytes=VMEM_BYTES),
        cost_estimate=pl.CostEstimate(
            flops=2 * rows * width * TENSOR * columns,
            bytes_accessed=2 * TENSOR * width * (rows + columns) + 2 * rows * columns,
            transcendentals=rows,
        ),
        name="project",
    )(order, group, *pieces, gain, w_query, w_key, w_value, q_bias, v_bias)


def attend_kernel(heads, first, parts, source, sequence, context, *refs):
    own, other = refs[:parts], refs[parts : 2 * parts]
    out, keys, values, best, total, summed = refs[2 * parts :]
    pages = own[0].shape[0]
    count = own[0].shape[1]
    key_at = own[0].shape[2] - 2 * HEAD
    half = pages * PAGE
    rows_q, rows_k = 2 * PAGE, 4 * PAGE
    blocks_half = half // rows_k
    factor = math.log2(math.e) / math.sqrt(HEAD)
    is_second = context[0]

    def place_page(slot, carry):
        for part in range(parts):
            at = pl.ds(pl.multiple_of(half + slot * PAGE + part * count, count), count)
            page = source[pages + slot]
            keys[at, :] = own[part][page, :, key_at : key_at + HEAD]
            values[at, :] = own[part][page, :, key_at + HEAD :]
            at = pl.ds(pl.multiple_of(slot * PAGE + part * count, count), count)
            page = source[slot]
            keys[at, :] = other[part][page, :, :HEAD]
            values[at, :] = other[part][page, :, HEAD:]
        return carry

    lax.fori_loop(0, pages, place_page, 0)

    def query_block(index, carry):
        slot = index * 2
        query = jnp.concatenate(
            [
                own[part][source[pages + slot + page], :, (first + head) * HEAD : (first + head + 1) * HEAD]
                for head in range(heads)
                for page in range(2)
                for part in range(parts)
            ],
            axis=0,
        )
        sequence_q = [sequence[pages + slot + page] for page in range(2)]

        def scores_of(block):
            at = pl.ds(pl.multiple_of(block * rows_k, rows_k), rows_k)
            scores = lax.dot_general(
                query, keys[at, :], (((1,), (1,)), ((), ())), preferred_element_type=jnp.float32
            )
            row = lax.broadcasted_iota(jnp.int32, (rows_q, rows_k), 0)
            column = lax.broadcasted_iota(jnp.int32, (rows_q, rows_k), 1)
            seq_row = jnp.where(row < PAGE, sequence_q[0], sequence_q[1])
            seq_column = jnp.full((rows_q, rows_k), sequence[block * 4 + 3], jnp.int32)
            for page in (2, 1, 0):
                seq_column = jnp.where(
                    column < (page + 1) * PAGE, sequence[block * 4 + page], seq_column
                )
            visible = (seq_row == seq_column) & (
                column + block * rows_k <= row + half + index * rows_q
            )
            scores = (scores * factor).reshape(heads, rows_q, rows_k)
            scores = jnp.where(visible[None], scores, -1e30)
            return scores.reshape(heads * rows_q, rows_k), values[at, :]

        diagonal = blocks_half + index // 2
        scores, value = scores_of(diagonal)
        top = jnp.max(scores, axis=1, keepdims=True)
        weight = jnp.exp2(scores - top)
        best[...] = top
        total[...] = jnp.sum(weight, axis=1, keepdims=True)
        summed[...] = jnp.dot(
            weight.astype(jnp.bfloat16), value, preferred_element_type=jnp.float32
        )

        def key_block(block, carry):
            seen = False
            for page in range(4):
                seq = sequence[block * 4 + page]
                seen = seen | (seq == sequence_q[0]) | (seq == sequence_q[1])

            @pl.when(seen)
            def _():
                scores, value = scores_of(block)
                top = jnp.maximum(best[...], jnp.max(scores, axis=1, keepdims=True))
                weight = jnp.exp2(scores - top)
                fade = jnp.exp2(best[...] - top)
                best[...] = top
                total[...] = total[...] * fade + jnp.sum(weight, axis=1, keepdims=True)
                summed[...] = summed[...] * fade + jnp.dot(
                    weight.astype(jnp.bfloat16), value, preferred_element_type=jnp.float32
                )

            return carry

        lax.fori_loop(jnp.where(is_second > 0, 0, blocks_half), diagonal, key_block, 0)
        result = (summed[...] / total[...]).astype(jnp.bfloat16)
        for head in range(heads):
            for page in range(2):
                start = head * rows_q + page * PAGE
                out[source[pages + slot + page], :, head * HEAD : (head + 1) * HEAD] = result[
                    start : start + PAGE
                ]
        return carry

    lax.fori_loop(0, pages // 2, query_block, 0)


def attend(heads, first, source, sequence, context, own, other):
    pages = own[0].shape[0]
    parts = len(own)

    def kernel(*refs):
        attend_kernel(heads, first, parts, *refs)

    rows = heads * 2 * PAGE
    half = pages * PAGE
    vmem = pl.BlockSpec(memory_space=pltpu.VMEM)
    smem = pl.BlockSpec(memory_space=pltpu.SMEM)
    return pl.pallas_call(
        kernel,
        out_shape=jax.ShapeDtypeStruct((pages, PAGE, heads * HEAD), jnp.bfloat16),
        in_specs=[smem] * 3 + [vmem] * (2 * parts),
        out_specs=vmem,
        scratch_shapes=[
            pltpu.VMEM((2 * half, HEAD), jnp.bfloat16),
            pltpu.VMEM((2 * half, HEAD), jnp.bfloat16),
            pltpu.VMEM((rows, 1), jnp.float32),
            pltpu.VMEM((rows, 1), jnp.float32),
            pltpu.VMEM((rows, HEAD), jnp.float32),
        ],
        compiler_params=pltpu.CompilerParams(vmem_limit_bytes=VMEM_BYTES),
        cost_estimate=pl.CostEstimate(
            flops=4 * half * half * HEAD * heads,
            bytes_accessed=2 * half * (own[0].shape[2] + 2 * HEAD + heads * HEAD),
            transcendentals=half * half * heads,
        ),
        name="attend",
    )(source, sequence, context, *own, *other)


def mix_kernel(final, heads, first, page_of, own, left, right, far_top, far_low, w_out, *refs):
    step = pl.program_id(1)
    last = pl.num_programs(1) - 1
    if final:
        hidden, before, out, total = refs
    else:
        out, total = refs
    band = w_out[...].reshape(-1, w_out.shape[-1])[first * HEAD : (first + heads) * HEAD]

    def product(piece):
        return jnp.dot(piece[...], band, preferred_element_type=jnp.float32)

    @pl.when(step == 0)
    def _():
        total[...] = product(own)

    for index, piece in ((1, left), (2, right)):

        @pl.when(step == index)
        def _(piece=piece):
            total[...] = total[...] + product(piece)

    @pl.when(step == last)
    def _():
        half = far_top.shape[0]
        for start, piece in ((0, far_top), (half, far_low)):
            sums = total[pl.ds(start, half)] + product(piece)
            if not final:
                out[pl.ds(start, half)] = sums
                continue
            sums = sums + before[pl.ds(start, half)]
            for index in range(half // PAGE):
                page = page_of[start // PAGE + index]
                rows = sums[index * PAGE : (index + 1) * PAGE]
                out[page] = (hidden[page].astype(jnp.float32) + rows).astype(jnp.bfloat16)


def mix(heads, first, page_of, pieces, w_out, hidden=None, before=None):
    rows = pieces[0].shape[0]
    outer, cuts, _, depth, columns = w_out.shape
    final = hidden is not None

    def kernel(*refs):
        mix_kernel(final, heads, first, *refs)

    def whole(a):
        return pl.BlockSpec(a.shape, lambda n, k, page_of: (0,) * a.ndim)

    paged = pl.BlockSpec((rows // PAGE, PAGE, columns), lambda n, k, page_of: (0, 0, n))
    flat = pl.BlockSpec((rows, columns), lambda n, k, page_of: (0, n))
    if final:
        extra, extra_specs = (hidden, before), [paged, flat]
        out_shape = jax.ShapeDtypeStruct(hidden.shape, jnp.bfloat16)
        out_spec = paged
    else:
        extra, extra_specs = (), []
        out_shape = jax.ShapeDtypeStruct((rows, cuts * columns), jnp.float32)
        out_spec = flat
    return pl.pallas_call(
        kernel,
        out_shape=out_shape,
        grid_spec=pltpu.PrefetchScalarGridSpec(
            num_scalar_prefetch=1,
            grid=(cuts, TENSOR),
            in_specs=[whole(p) for p in pieces]
            + [
                pl.BlockSpec(
                    (outer, 1, 1, depth, columns), lambda n, k, page_of: (0, n, k, 0, 0)
                )
            ]
            + extra_specs,
            out_specs=out_spec,
            scratch_shapes=[pltpu.VMEM((rows, columns), jnp.float32)],
        ),
        compiler_params=pltpu.CompilerParams(vmem_limit_bytes=VMEM_BYTES),
        cost_estimate=pl.CostEstimate(
            flops=2 * rows * heads * HEAD * TENSOR * cuts * columns,
            bytes_accessed=2 * w_out.size + 6 * rows * cuts * columns,
            transcendentals=0,
        ),
        name="mix",
    )(page_of, *pieces, w_out, *extra)


def recut(w_out, context, outer_index, outer):
    depth = w_out.shape[0] // outer
    columns = w_out.shape[1] // (2 * TENSOR)
    band = lax.dynamic_slice_in_dim(w_out, outer_index * depth, depth, 0)
    me = lax.axis_index("tensor")

    def cut(step):
        target = (me + step) % TENSOR
        return lax.dynamic_slice_in_dim(band, (target * 2 + context) * columns, columns, 1)

    def shift(step):
        return [(i, (i + step) % TENSOR) for i in range(TENSOR)]

    pieces = [
        cut(0),
        lax.ppermute(cut(1), "tensor", shift(1)),
        lax.ppermute(cut(3), "tensor", shift(3)),
        lax.ppermute(cut(2), "tensor", shift(2)),
    ]
    whole = lax.all_gather(jnp.stack(pieces), ("z", "xh", "context"), axis=0, tiled=False)
    return whole.reshape(outer, 2, TENSOR, depth, columns)


def body(hidden, seq_id, dest_page, norm_gain, w_query, q_bias, w_key, w_value, v_bias, w_out):
    pages = dest_page.shape[0]
    me = lax.axis_index("tensor")
    context = lax.axis_index("context")
    group = dest_page // pages
    order = jnp.stack([me, (me + 3) % TENSOR, (me + 1) % TENSOR, (me + 2) % TENSOR]).astype(jnp.int32)

    paged = hidden.reshape(pages, PAGE, hidden.shape[1])
    gathered = [
        ring_gather(paged[:, at : at + STEP].reshape(pages * STEP, -1))
        for at in range(0, PAGE, STEP)
    ]
    w_all = recut(w_out, context, lax.axis_index(("z", "xh")), 8)

    facts = jnp.concatenate([dest_page, seq_id[::PAGE]])
    facts, _ = lax.optimization_barrier((facts, gathered[0][1]))
    facts = lax.all_gather(facts, DP + ("context",), axis=0, tiled=False)
    facts = facts.reshape(-1, 2, 2, pages)
    mine = lax.axis_index(DP)
    slots = jnp.arange(pages, dtype=jnp.int32)
    hit = facts[:, :, 0, None, :] == (mine * pages + slots)[None, None, :, None]
    owners = jnp.arange(facts.shape[0], dtype=jnp.int32)
    source = jnp.sum(jnp.where(hit, owners[:, None, None, None], 0), axis=(0, 3))
    sequence = jnp.sum(jnp.where(hit, facts[:, :, 1, None, :], 0), axis=(0, 3))
    source = jnp.concatenate([source[0], jnp.where(context > 0, source[1], source[0])])
    sequence = jnp.concatenate([sequence[0], jnp.where(context > 0, sequence[1], sequence[0])])
    page_of = jnp.sum(jnp.where(group[None, :] == slots[:, None], slots[None, :], 0), axis=1)

    own, other = [], []
    for pieces in gathered:
        rows = project(order, group, pieces, norm_gain, w_query, w_key, w_value, q_bias, v_bias)
        rows = lax.all_to_all(rows, DP, split_axis=0, concat_axis=0, tiled=True)
        own.append(rows)
        other.append(lax.ppermute(rows[:, :, w_query.shape[1] :], "context", [(0, 1)]))

    heads = w_query.shape[1] // HEAD
    cuts = [(0, 3), (3, heads)]
    second = context.astype(jnp.int32).reshape(1)
    total = None
    for first, end in cuts:
        part = attend(end - first, first, source, sequence, second, own, other)
        part = lax.all_to_all(part, DP, split_axis=0, concat_axis=0, tiled=True)
        pieces = ring_gather(part.reshape(pages * PAGE, -1))
        if end < heads:
            total = mix(end - first, first, page_of, pieces, w_all)
        else:
            result = mix(end - first, first, page_of, pieces, w_all, paged, total)
    return result.reshape(hidden.shape)


def solution(mesh):
    fine = Mesh(
        mesh.devices.reshape(4, 2, 2, 2, TENSOR), ("z", "xh", "core", "context", "tensor")
    )
    rows = DP + ("context",)
    return jax.shard_map(
        body,
        mesh=fine,
        in_specs=(
            P(rows, "tensor"),
            P(rows),
            P(rows),
            P(),
            P(None, "tensor"),
            P("tensor"),
            P(None, "tensor"),
            P(None, "tensor"),
            P("tensor"),
            P("tensor", None),
        ),
        out_specs=P(rows, "tensor"),
        check_vma=False,
    )
```

```python
import math

import jax
import jax.numpy as jnp
from jax import lax
from jax.experimental import pallas as pl
from jax.experimental.pallas import tpu as pltpu
from jax.sharding import Mesh
from jax.sharding import PartitionSpec as P

HEAD = 128
PAGE = 64
EPSILON = 1e-06
DP = ("z", "xh", "core")
TENSOR = 4
PARTS = ((0, 32), (32, 48), (48, 64))
FACTS = 128
DIGIT = 32
MIB = 1024 * 1024


def ring_gather(block):
    right = [(i, (i + 1) % TENSOR) for i in range(TENSOR)]
    left = [(i, (i - 1) % TENSOR) for i in range(TENSOR)]
    half = block.shape[0] // 2
    from_left = lax.ppermute(block, "tensor", right)
    from_right = lax.ppermute(block, "tensor", left)
    far_top = lax.ppermute(from_left[:half], "tensor", right)
    far_low = lax.ppermute(from_right[half:], "tensor", left)
    return (block, from_left, from_right, far_top, far_low)


def project_kernel(steps, first, final, facts, counts, order, page, *refs):
    refs = list(refs)
    pieces = [[refs.pop(0) for _ in range(count)] for count in counts]
    gain, weights = refs.pop(0), refs.pop(0)
    if not first:
        total_in, squares_in = refs.pop(0), refs.pop(0)
    if final:
        bias, out, total, squares = refs
    else:
        total, squares = refs
    step = pl.program_id(0)

    for index in range(steps):

        @pl.when(step == index)
        def _(index=index):
            start = 0
            for piece in pieces[index]:
                at = pl.ds(start, piece.shape[0])
                start += piece.shape[0]
                wide = piece[...].astype(jnp.float32)
                square = jnp.sum(wide * wide, axis=1, keepdims=True)
                scaled = (wide * gain[0].astype(jnp.float32)).astype(jnp.bfloat16)
                product = jnp.dot(scaled, weights[...], preferred_element_type=jnp.float32)
                if index == 0 and first:
                    total[at], squares[at] = product, square
                elif index == 0:
                    total[at], squares[at] = total_in[at] + product, squares_in[at] + square
                else:
                    total[at], squares[at] = total[at] + product, squares[at] + square

    if not final:
        return

    @pl.when(step == steps - 1)
    def _():
        features = TENSOR * pieces[0][0].shape[1]
        scale = lax.rsqrt(squares[...] * (1.0 / features) + EPSILON)
        result = (total[...] * scale + bias[...]).astype(jnp.bfloat16)
        pages, count, columns = out.shape
        columns = result.shape[1]
        for index in range(pages):
            target = page[index]
            out[target, :, :columns] = result[index * count : (index + 1) * count]
            if facts:
                lane = lax.broadcasted_iota(jnp.int32, (count, FACTS), 1)
                fact = jnp.where(
                    lane == 0,
                    page[pages + index],
                    jnp.where(
                        lane == 1,
                        page[2 * pages + index],
                        jnp.where(lane == 2, page[3 * pages + index], 0),
                    ),
                )
                out[target, :, columns:] = fact.astype(jnp.float32).astype(jnp.bfloat16)


def project(order, page, pieces, first, gain, weights, bias, carry=None, facts=False):
    steps = len(pieces)
    final = first + steps == TENSOR
    rows = sum(p.shape[0] for p in pieces[0])
    width, columns = pieces[0][0].shape[1], weights.shape[1]
    pages = page.shape[0] // 4
    counts = [len(group) for group in pieces]

    def kernel(*refs):
        project_kernel(steps, carry is None, final, facts, counts, *refs)

    def whole(shape):
        return pl.BlockSpec(shape, lambda k, order, page: (0,) * len(shape))

    operands = [p for group in pieces for p in group]
    in_specs = [whole(p.shape) for p in operands]
    operands += [gain.reshape(TENSOR, 1, width), weights]
    in_specs += [
        pl.BlockSpec((1, 1, width), lambda k, order, page: (order[first + k], 0, 0)),
        pl.BlockSpec((width, columns), lambda k, order, page: (order[first + k], 0)),
    ]
    if carry is not None:
        operands += list(carry)
        in_specs += [whole(c.shape) for c in carry]
    sums = [(rows, columns), (rows, 1)]
    if final:
        operands.append(bias)
        in_specs.append(whole(bias.shape))
        shape = (pages, rows // pages, columns + (FACTS if facts else 0))
        out_shape = jax.ShapeDtypeStruct(shape, jnp.bfloat16)
        out_specs = whole(shape)
        scratch = [pltpu.VMEM(shape, jnp.float32) for shape in sums]
    else:
        out_shape = [jax.ShapeDtypeStruct(shape, jnp.float32) for shape in sums]
        out_specs = [whole(shape) for shape in sums]
        scratch = []
    return pl.pallas_call(
        kernel,
        out_shape=out_shape,
        grid_spec=pltpu.PrefetchScalarGridSpec(
            num_scalar_prefetch=2,
            grid=(steps,),
            in_specs=in_specs,
            out_specs=out_specs,
            scratch_shapes=scratch,
        ),
        compiler_params=pltpu.CompilerParams(vmem_limit_bytes=36 * MIB),
        cost_estimate=pl.CostEstimate(
            flops=4 * rows * width * steps * columns,
            bytes_accessed=2 * steps * width * (rows + columns) + 2 * rows * columns,
            transcendentals=rows,
        ),
        name="project",
    )(order, page, *operands)


def attend_kernel(heads, first, parts, source, sequence, context, *refs):
    own, other = refs[:parts], refs[parts : 2 * parts]
    out, keys, values, turned, best, total, summed = refs[2 * parts :]
    pages = own[0].shape[0]
    key_at = own[-1].shape[2] - 2 * HEAD
    half = pages * PAGE
    per = 4
    rows = per * PAGE
    blocks = pages // per
    lanes = heads * rows
    factor = math.log2(math.e) / math.sqrt(HEAD)

    def place_page(slot, carry):
        start = 0
        for part in range(parts):
            count = own[part].shape[1]
            at = pl.ds(pl.multiple_of(half + slot * PAGE + start, 16), count)
            page = source[pages + slot]
            keys[at, :] = own[part][page, :, key_at : key_at + HEAD]
            values[at, :] = own[part][page, :, key_at + HEAD : key_at + 2 * HEAD]
            at = pl.ds(pl.multiple_of(slot * PAGE + start, 16), count)
            page = source[slot]
            keys[at, :] = other[part][page, :, :HEAD]
            values[at, :] = other[part][page, :, HEAD : 2 * HEAD]
            start += count
        return carry

    lax.fori_loop(0, pages, place_page, 0)
    for block in range(2 * blocks):
        turned[block] = values[pl.ds(block * rows, rows), :].astype(jnp.float32).T.astype(jnp.bfloat16)

    def query_block(index, carry):
        slot = index * per
        query = jnp.concatenate(
            [
                own[part][source[pages + slot + page], :, (first + head) * HEAD : (first + head + 1) * HEAD]
                for head in range(heads)
                for page in range(per)
                for part in range(parts)
            ],
            axis=0,
        )
        sequence_q = [sequence[pages + slot + page] for page in range(per)]
        within = lax.broadcasted_iota(jnp.int32, (1, lanes), 1) % rows
        seq_lane = jnp.full((1, lanes), sequence_q[per - 1], jnp.int32)
        for page in range(per - 2, -1, -1):
            seq_lane = jnp.where(within < (page + 1) * PAGE, sequence_q[page], seq_lane)

        def scores_of(block, diagonal):
            at = pl.ds(pl.multiple_of(block * rows, rows), rows)
            scores = lax.dot_general(
                keys[at, :], query, (((1,), (1,)), ((), ())), preferred_element_type=jnp.float32
            )
            cut = []
            for page in range(per):
                visible = seq_lane == sequence[block * per + page]
                if diagonal:
                    place = lax.broadcasted_iota(jnp.int32, (PAGE, lanes), 0) + page * PAGE
                    visible = visible & (place <= within)
                cut.append(jnp.where(visible, scores[page * PAGE : (page + 1) * PAGE], -1e30))
            return jnp.concatenate(cut, axis=0)

        def apply(block, weight):
            return jnp.dot(
                turned[block], weight.astype(jnp.bfloat16), preferred_element_type=jnp.float32
            )

        last = blocks + index
        scores = scores_of(last, True)
        top = jnp.max(scores, axis=0, keepdims=True)
        weight = jnp.exp2((scores - top) * factor)
        best[...] = top
        total[...] = jnp.sum(weight, axis=0, keepdims=True)
        summed[...] = apply(last, weight)

        def key_block(block, carry):
            seen = False
            for page in range(per):
                for seq in sequence_q:
                    seen = seen | (sequence[block * per + page] == seq)

            @pl.when(seen)
            def _():
                scores = scores_of(block, False)
                top = jnp.maximum(best[...], jnp.max(scores, axis=0, keepdims=True))
                weight = jnp.exp2((scores - top) * factor)
                fade = jnp.exp2((best[...] - top) * factor)
                best[...] = top
                total[...] = total[...] * fade + jnp.sum(weight, axis=0, keepdims=True)
                summed[...] = summed[...] * fade + apply(block, weight)

            return carry

        lax.fori_loop(jnp.where(context[0] > 0, 0, blocks), last, key_block, 0)
        result = (summed[...] / total[...]).T.astype(jnp.bfloat16)
        for head in range(heads):
            for page in range(per):
                start = head * rows + page * PAGE
                out[source[pages + slot + page], :, head * HEAD : (head + 1) * HEAD] = result[
                    start : start + PAGE
                ]
        return carry

    lax.fori_loop(0, blocks, query_block, 0)


def attend(heads, first, source, sequence, context, own, other):
    pages = own[0].shape[0]
    parts = len(own)

    def kernel(*refs):
        attend_kernel(heads, first, parts, *refs)

    half = pages * PAGE
    lanes = heads * 4 * PAGE
    vmem = pl.BlockSpec(memory_space=pltpu.VMEM)
    smem = pl.BlockSpec(memory_space=pltpu.SMEM)
    return pl.pallas_call(
        kernel,
        out_shape=jax.ShapeDtypeStruct((pages, PAGE, heads * HEAD), jnp.bfloat16),
        in_specs=[smem] * 3 + [vmem] * (2 * parts),
        out_specs=vmem,
        scratch_shapes=[
            pltpu.VMEM((2 * half, HEAD), jnp.bfloat16),
            pltpu.VMEM((2 * half, HEAD), jnp.bfloat16),
            pltpu.VMEM((pages // 2, HEAD, 4 * PAGE), jnp.bfloat16),
            pltpu.VMEM((1, lanes), jnp.float32),
            pltpu.VMEM((1, lanes), jnp.float32),
            pltpu.VMEM((HEAD, lanes), jnp.float32),
        ],
        compiler_params=pltpu.CompilerParams(vmem_limit_bytes=24 * MIB),
        cost_estimate=pl.CostEstimate(
            flops=4 * half * half * HEAD * heads,
            bytes_accessed=2 * half * (own[0].shape[2] + 2 * HEAD + heads * HEAD),
            transcendentals=half * half * heads,
        ),
        name="attend",
    )(source, sequence, context, *own, *other)


def mix_kernel(steps, rows_at, depth, final, counts, carried, page_of, *refs):
    refs = list(refs)
    pieces = [[refs.pop(0) for _ in range(count)] for count in counts]
    w_out = refs.pop(0)
    before = refs.pop(0) if carried else None
    if final:
        hidden, out, total = refs
    else:
        (total,) = refs
    step = pl.program_id(1)
    band = w_out[:, 0, 0, rows_at : rows_at + depth, :].reshape(-1, w_out.shape[-1])

    for index in range(steps):

        @pl.when(step == index)
        def _(index=index):
            start = 0
            for piece in pieces[index]:
                at = pl.ds(start, piece.shape[0])
                product = jnp.dot(piece[...], band, preferred_element_type=jnp.float32)
                if index > 0:
                    product = total[at] + product
                elif carried:
                    product = before[at] + product
                if not (final and index == steps - 1):
                    total[at] = product
                else:
                    for item in range(piece.shape[0] // PAGE):
                        page = page_of[start // PAGE + item]
                        rows = product[item * PAGE : (item + 1) * PAGE]
                        out[page] = (hidden[page].astype(jnp.float32) + rows).astype(jnp.bfloat16)
                start += piece.shape[0]


def mix(page_of, pieces, first, w_out, rows_at, depth, before=None, hidden=None):
    steps = len(pieces)
    rows = sum(p.shape[0] for p in pieces[0])
    outer, cuts, _, stored, columns = w_out.shape
    final, carried = hidden is not None, before is not None
    counts = [len(group) for group in pieces]

    def kernel(*refs):
        mix_kernel(steps, rows_at, depth, final, counts, carried, *refs)

    paged = pl.BlockSpec((rows // PAGE, PAGE, columns), lambda n, k, page_of: (0, 0, n))
    flat = pl.BlockSpec((rows, columns), lambda n, k, page_of: (0, n))
    operands = [p for group in pieces for p in group]
    in_specs = [pl.BlockSpec(p.shape, lambda n, k, page_of: (0, 0)) for p in operands]
    operands.append(w_out)
    in_specs.append(
        pl.BlockSpec(
            (outer, 1, 1, stored, columns), lambda n, k, page_of: (0, n, first + k, 0, 0)
        )
    )
    if carried:
        operands.append(before)
        in_specs.append(flat)
    if final:
        operands.append(hidden)
        in_specs.append(paged)
        out_shape = jax.ShapeDtypeStruct(hidden.shape, jnp.bfloat16)
        out_spec = paged
        scratch = [pltpu.VMEM((rows, columns), jnp.float32)]
    else:
        out_shape = jax.ShapeDtypeStruct((rows, cuts * columns), jnp.float32)
        out_spec = flat
        scratch = []
    return pl.pallas_call(
        kernel,
        out_shape=out_shape,
        grid_spec=pltpu.PrefetchScalarGridSpec(
            num_scalar_prefetch=1,
            grid=(cuts, steps),
            in_specs=in_specs,
            out_specs=out_spec,
            scratch_shapes=scratch,
        ),
        compiler_params=pltpu.CompilerParams(vmem_limit_bytes=40 * MIB),
        cost_estimate=pl.CostEstimate(
            flops=4 * rows * outer * depth * steps * cuts * columns,
            bytes_accessed=2 * outer * depth * steps * cuts * columns + 6 * rows * cuts * columns,
            transcendentals=0,
        ),
        name="mix",
    )(page_of, *operands)


def recut(w_out, context, outer_index, outer, cuts):
    columns = w_out.shape[1] // (2 * TENSOR)
    bands = []
    for first, end in cuts:
        depth = (end - first) * HEAD // outer
        bands.append(
            lax.dynamic_slice_in_dim(w_out, first * HEAD + outer_index * depth, depth, 0)
        )
    band = jnp.concatenate(bands, axis=0)
    me = lax.axis_index("tensor")

    def cut(step):
        target = (me + step) % TENSOR
        return lax.dynamic_slice_in_dim(band, (target * 2 + context) * columns, columns, 1)

    def shift(step):
        return [(i, (i + step) % TENSOR) for i in range(TENSOR)]

    pieces = [
        cut(0),
        lax.ppermute(cut(1), "tensor", shift(1)),
        lax.ppermute(cut(3), "tensor", shift(3)),
        lax.ppermute(cut(2), "tensor", shift(2)),
    ]
    whole = lax.all_gather(jnp.stack(pieces), ("z", "xh", "context"), axis=0, tiled=False)
    return whole.reshape(outer, 2, TENSOR, band.shape[0], columns)


def places(local, sequence):
    pages = local.shape[0]
    ladder = jnp.arange(pages, dtype=jnp.int32)
    hit = local[None, :] == ladder[:, None]
    source = jnp.sum(jnp.where(hit, ladder[None, :], 0), axis=1)
    return jnp.stack([source, jnp.sum(jnp.where(hit, sequence[None, :], 0), axis=1)])


def read_facts(facts):
    facts = facts.astype(jnp.float32).astype(jnp.int32)
    return places(facts[:, 0], facts[:, 1] * DIGIT + facts[:, 2])


def body(hidden, seq_id, dest_page, norm_gain, w_query, q_bias, w_key, w_value, v_bias, w_out):
    pages = dest_page.shape[0]
    me = lax.axis_index("tensor")
    context = lax.axis_index("context")
    heads = w_query.shape[1] // HEAD
    cuts = [(0, 3), (3, heads)]
    order = jnp.stack([me, (me + 3) % TENSOR, (me + 1) % TENSOR, (me + 2) % TENSOR]).astype(jnp.int32)
    sequence = seq_id[::PAGE]
    group = dest_page // pages
    page = jnp.concatenate([group, dest_page % pages, sequence // DIGIT, sequence % DIGIT])
    slots = jnp.arange(pages, dtype=jnp.int32)
    page_of = jnp.sum(jnp.where(group[None, :] == slots[:, None], slots[None, :], 0), axis=1)

    paged = hidden.reshape(pages, PAGE, hidden.shape[1])
    gathered = [
        ring_gather(paged[:, at:end].reshape(pages * (end - at), -1)) for at, end in PARTS
    ]
    w_out, _ = lax.optimization_barrier((w_out, gathered[0][1]))
    w_all = recut(w_out, context, lax.axis_index(("z", "xh")), 8, cuts)

    weights = jnp.concatenate([w_query, w_key, w_value], axis=1)
    bias = jnp.concatenate([q_bias, jnp.zeros_like(v_bias), v_bias]).astype(jnp.float32)[None, :]
    own, other = [], []
    for index, (mine, left, right, top, low) in enumerate(gathered):
        facts = index == 0
        if index < len(PARTS) - 1:
            pieces = [(mine,), (left,), (right,), (top, low)]
            rows = project(order, page, pieces, 0, norm_gain, weights, bias, facts=facts)
        else:
            carry = project(order, page, [(mine,), (left,), (right,)], 0, norm_gain, weights, bias)
            rows = project(order, page, [(top, low)], 3, norm_gain, weights, bias, carry, facts)
        rows = lax.all_to_all(rows, DP, split_axis=0, concat_axis=0, tiled=True)
        own.append(rows)
        other.append(lax.ppermute(rows[:, :, w_query.shape[1] :], "context", [(0, 1)]))

    at = weights.shape[1]
    here = read_facts(own[0][:, 0, at : at + 3])
    there = read_facts(other[0][:, 0, 2 * HEAD : 2 * HEAD + 3])
    there = jnp.where(context > 0, there, here)
    source = jnp.concatenate([there[0], here[0]])
    sequence = jnp.concatenate([there[1], here[1]])

    second = context.astype(jnp.int32).reshape(1)
    parts = []
    for first, end in cuts:
        parts.append(attend(end - first, first, source, sequence, second, own, other))
    exchanged = [
        lax.all_to_all(part, DP, split_axis=0, concat_axis=0, tiled=True) for part in parts
    ]
    exchanged[0], _ = lax.optimization_barrier((exchanged[0], parts[1]))
    total, rows_at = None, 0
    for index, (first, end) in enumerate(cuts):
        depth = (end - first) * HEAD // 8
        mine, left, right, top, low = ring_gather(exchanged[index].reshape(pages * PAGE, -1))
        if end < heads:
            pieces = [(mine,), (left,), (right,), (top, low)]
            total = mix(page_of, pieces, 0, w_all, rows_at, depth)
        else:
            pieces = [(mine,), (left,), (right,)]
            total = mix(page_of, pieces, 0, w_all, rows_at, depth, total)
            result = mix(page_of, [(top, low)], 3, w_all, rows_at, depth, total, paged)
        rows_at += depth
    return result.reshape(hidden.shape)


def solution(mesh):
    fine = Mesh(
        mesh.devices.reshape(4, 2, 2, 2, TENSOR), ("z", "xh", "core", "context", "tensor")
    )
    rows = DP + ("context",)
    return jax.shard_map(
        body,
        mesh=fine,
        in_specs=(
            P(rows, "tensor"),
            P(rows),
            P(rows),
            P(),
            P(None, "tensor"),
            P("tensor"),
            P(None, "tensor"),
            P(None, "tensor"),
            P("tensor"),
            P("tensor", None),
        ),
        out_specs=P(rows, "tensor"),
        check_vma=False,
    )
```

```python
import math

import jax
import jax.numpy as jnp
from jax import lax
from jax.experimental import pallas as pl
from jax.experimental.pallas import tpu as pltpu
from jax.sharding import Mesh
from jax.sharding import PartitionSpec as P

HEAD = 128
PAGE = 64
EPSILON = 1e-06
DP = ("z", "xh", "core")
TENSOR = 4
FACTS = 128
DIGIT = 32
MIB = 1024 * 1024
SMALL = pl.CostEstimate(flops=1024, bytes_accessed=1024, transcendentals=0)


def to_right(block):
    return lax.ppermute(block, "tensor", [(i, (i + 1) % TENSOR) for i in range(TENSOR)])


def to_left(block):
    return lax.ppermute(block, "tensor", [(i, (i - 1) % TENSOR) for i in range(TENSOR)])


def ring_near(top, low):
    return (to_right(top), to_right(low)), (to_left(top), to_left(low))


def ring_far(left, right):
    return to_right(left), to_left(right)


def project_near_kernel(count, *refs):
    pieces, weights, gains = refs[: 2 * count], refs[2 * count : 3 * count], refs[3 * count]
    total, squares = refs[3 * count + 1 :]
    step = pl.program_id(0)
    for index in range(count):

        @pl.when(step == index)
        def _(index=index):
            for half in range(2):
                piece = pieces[2 * index + half]
                at = pl.ds(half * piece.shape[0], piece.shape[0])
                product, square = banded(piece, gains[index], weights[index])
                if index == 0:
                    total[at], squares[at] = product, square
                else:
                    total[at], squares[at] = total[at] + product, squares[at] + square


def banded(piece, gain, weights):
    wide = piece[...].astype(jnp.float32)
    scaled = (wide * gain.astype(jnp.float32)).astype(jnp.bfloat16)
    product = jnp.dot(scaled, weights[...], preferred_element_type=jnp.float32)
    return product, jnp.sum(wide * wide, axis=1, keepdims=True)


def project_near(pieces, weights, gains):
    count = len(pieces)
    half, width = pieces[0][0].shape
    rows = 2 * half
    pieces = [half for piece in pieces for half in piece]
    columns = weights[0].shape[1]
    sums = [(rows, columns), (rows, 1)]

    def kernel(*refs):
        project_near_kernel(count, *refs)

    def whole(shape):
        return pl.BlockSpec(shape, lambda k: (0,) * len(shape))

    return pl.pallas_call(
        kernel,
        out_shape=[jax.ShapeDtypeStruct(shape, jnp.float32) for shape in sums],
        grid=(count,),
        in_specs=[whole((half, width)) for _ in pieces]
        + [whole(a.shape) for a in (*weights, gains)],
        out_specs=[whole(shape) for shape in sums],
        compiler_params=pltpu.CompilerParams(vmem_limit_bytes=56 * MIB),
        cost_estimate=SMALL,
        name="project_near",
    )(*pieces, *weights, gains)


def project_far_kernel(blocks, page, top, low, weights, gain, bias, total, squares, queries, others):
    step = pl.program_id(0)
    pages, count, heads_wide = queries.shape
    columns = weights.shape[1]
    features = TENSOR * top.shape[1]

    def finish(piece):
        product, square = banded(piece, gain[0], weights)
        scale = lax.rsqrt((squares[...] + square) * (1.0 / features) + EPSILON)
        result = ((total[...] + product) * scale + bias[...]).astype(jnp.bfloat16)
        for item in range(pages // blocks):
            index = step * (pages // blocks) + item
            target = page[index]
            rows = result[item * count : (item + 1) * count]
            queries[target] = rows[:, :heads_wide]
            others[target, :, : columns - heads_wide] = rows[:, heads_wide:]
            lane = lax.broadcasted_iota(jnp.int32, (count, FACTS), 1)
            fact = jnp.zeros_like(lane)
            for place in range(3):
                fact = jnp.where(lane == place, page[(place + 1) * pages + index], fact)
            others[target, :, columns - heads_wide :] = fact.astype(jnp.float32).astype(jnp.bfloat16)

    pl.when(step < blocks // 2)(lambda: finish(top))
    pl.when(step >= blocks // 2)(lambda: finish(low))


def project_far(page, top, low, weights, gain, bias, carry, heads_wide):
    blocks = 4
    half, width = carry[0].shape[0] // 2, top.shape[1]
    columns = weights.shape[1]
    pages = page.shape[0] // 4
    block = 2 * half // blocks
    shapes = [
        (pages, 2 * half // pages, wide) for wide in (heads_wide, columns - heads_wide + FACTS)
    ]

    def kernel(*refs):
        project_far_kernel(blocks, *refs)

    def whole(shape):
        return pl.BlockSpec(shape, lambda r, page: (0,) * len(shape))

    return pl.pallas_call(
        kernel,
        out_shape=[jax.ShapeDtypeStruct(shape, jnp.bfloat16) for shape in shapes],
        grid_spec=pltpu.PrefetchScalarGridSpec(
            num_scalar_prefetch=1,
            grid=(blocks,),
            in_specs=[
                pl.BlockSpec((block, width), lambda r, page: (jnp.minimum(r, blocks // 2 - 1), 0)),
                pl.BlockSpec((block, width), lambda r, page: (jnp.maximum(r - blocks // 2, 0), 0)),
                whole(weights.shape),
                whole(gain.shape),
                whole(bias.shape),
                pl.BlockSpec((block, columns), lambda r, page: (r, 0)),
                pl.BlockSpec((block, 1), lambda r, page: (r, 0)),
            ],
            out_specs=[whole(shape) for shape in shapes],
        ),
        compiler_params=pltpu.CompilerParams(vmem_limit_bytes=28 * MIB),
        cost_estimate=SMALL,
        name="project_far",
    )(page, top, low, weights, gain, bias, *carry)


def attend_kernel(heads, first, source, sequence, context, queries, own, other, out, *scratch):
    keys, values, turned, best, total, summed = scratch
    pages = own.shape[0]
    half = pages * PAGE
    per = 4
    rows = per * PAGE
    blocks = pages // per
    lanes = heads * rows
    factor = math.log2(math.e) / math.sqrt(HEAD)

    def place_page(slot, carry):
        for base, lookup, array in ((0, 0, other), (half, pages, own)):
            page = source[lookup + slot]
            at = pl.ds(pl.multiple_of(base + slot * PAGE, PAGE), PAGE)
            keys[at, :] = array[page, :, :HEAD]
            values[at, :] = array[page, :, HEAD : 2 * HEAD]
        return carry

    lax.fori_loop(0, pages, place_page, 0)
    for block in range(2 * blocks):
        turned[block] = values[pl.ds(block * rows, rows), :].astype(jnp.float32).T.astype(jnp.bfloat16)

    def query_block(index, carry):
        slot = index * per
        query = jnp.concatenate(
            [
                queries[source[pages + slot + page], :, (first + head) * HEAD : (first + head + 1) * HEAD]
                for head in range(heads)
                for page in range(per)
            ],
            axis=0,
        )
        sequence_q = [sequence[pages + slot + page] for page in range(per)]
        within = lax.broadcasted_iota(jnp.int32, (1, lanes), 1) % rows
        seq_lane = jnp.full((1, lanes), sequence_q[per - 1], jnp.int32)
        for page in range(per - 2, -1, -1):
            seq_lane = jnp.where(within < (page + 1) * PAGE, sequence_q[page], seq_lane)

        def scores_of(block, diagonal):
            at = pl.ds(pl.multiple_of(block * rows, rows), rows)
            scores = lax.dot_general(
                keys[at, :], query, (((1,), (1,)), ((), ())), preferred_element_type=jnp.float32
            )
            cut = []
            for page in range(per):
                visible = seq_lane == sequence[block * per + page]
                if diagonal:
                    place = lax.broadcasted_iota(jnp.int32, (PAGE, lanes), 0) + page * PAGE
                    visible = visible & (place <= within)
                cut.append(jnp.where(visible, scores[page * PAGE : (page + 1) * PAGE], -1e30))
            return jnp.concatenate(cut, axis=0)

        def apply(block, weight):
            return jnp.dot(
                turned[block], weight.astype(jnp.bfloat16), preferred_element_type=jnp.float32
            )

        last = blocks + index
        scores = scores_of(last, True)
        top = jnp.max(scores, axis=0, keepdims=True)
        weight = jnp.exp2((scores - top) * factor)
        best[...] = top
        total[...] = jnp.sum(weight, axis=0, keepdims=True)
        summed[...] = apply(last, weight)

        def key_block(block, carry):
            seen = False
            for page in range(per):
                for seq in sequence_q:
                    seen = seen | (sequence[block * per + page] == seq)

            @pl.when(seen)
            def _():
                scores = scores_of(block, False)
                top = jnp.maximum(best[...], jnp.max(scores, axis=0, keepdims=True))
                weight = jnp.exp2((scores - top) * factor)
                fade = jnp.exp2((best[...] - top) * factor)
                best[...] = top
                total[...] = total[...] * fade + jnp.sum(weight, axis=0, keepdims=True)
                summed[...] = summed[...] * fade + apply(block, weight)

            return carry

        lax.fori_loop(jnp.where(context[0] > 0, 0, blocks), last, key_block, 0)
        result = (summed[...] / total[...]).T.astype(jnp.bfloat16)
        for head in range(heads):
            for page in range(per):
                start = head * rows + page * PAGE
                out[source[pages + slot + page], :, head * HEAD : (head + 1) * HEAD] = result[
                    start : start + PAGE
                ]
        return carry

    lax.fori_loop(0, blocks, query_block, 0)


def attend(heads, first, source, sequence, context, queries, own, other):
    pages = own.shape[0]

    def kernel(*refs):
        attend_kernel(heads, first, *refs)

    half = pages * PAGE
    lanes = heads * 4 * PAGE
    vmem = pl.BlockSpec(memory_space=pltpu.VMEM)
    smem = pl.BlockSpec(memory_space=pltpu.SMEM)
    return pl.pallas_call(
        kernel,
        out_shape=jax.ShapeDtypeStruct((pages, PAGE, heads * HEAD), jnp.bfloat16),
        in_specs=[smem] * 3 + [vmem] * 3,
        out_specs=vmem,
        scratch_shapes=[
            pltpu.VMEM((2 * half, HEAD), jnp.bfloat16),
            pltpu.VMEM((2 * half, HEAD), jnp.bfloat16),
            pltpu.VMEM((pages // 2, HEAD, 4 * PAGE), jnp.bfloat16),
            pltpu.VMEM((1, lanes), jnp.float32),
            pltpu.VMEM((1, lanes), jnp.float32),
            pltpu.VMEM((HEAD, lanes), jnp.float32),
        ],
        compiler_params=pltpu.CompilerParams(vmem_limit_bytes=20 * MIB),
        cost_estimate=SMALL,
        name="attend",
    )(source, sequence, context, queries, own, other)


def rows_of(w_out, cut):
    begin, end = cut
    return w_out[:, 0, 0, begin:end, :].reshape(-1, w_out.shape[-1])


def mix_near_kernel(steps, counts, carried, paged, page_of, me, *refs):
    refs = list(refs)
    pieces = [[refs.pop(0) for _ in range(count)] for count in counts]
    w_own, w_all = refs.pop(0), refs.pop(0)
    before = refs.pop(0) if carried else None
    hidden = refs.pop(0) if paged else None
    (total,) = refs
    step = pl.program_id(1)

    for index, (place, cut) in enumerate(steps):

        @pl.when(step == index)
        def _(index=index, place=place, cut=cut):
            if place == 0:
                band = w_own[8 * cut[0] : 8 * cut[1], :]
            else:
                band = rows_of(w_all, cut)
            start = 0
            for piece in pieces[index]:
                count = piece.shape[0]
                at = pl.ds(start, count)
                product = jnp.dot(piece[...], band, preferred_element_type=jnp.float32)
                if index > 0:
                    product = total[at] + product
                elif carried:
                    product = before[at] + product
                if index == len(steps) - 1 and paged:
                    rows = [hidden[page_of[(start + k) // PAGE]] for k in range(0, count, PAGE)]
                    product = product + jnp.concatenate(rows, axis=0).astype(jnp.float32)
                total[at] = product
                start += count


def mix_near(page_of, me, pieces, steps, w_out, w_all, before=None, hidden=None):
    rows = sum(p.shape[0] for p in pieces[0])
    outer, cuts, _, stored, columns = w_all.shape
    counts = [len(group) for group in pieces]

    def kernel(*refs):
        mix_near_kernel(steps, counts, before is not None, hidden is not None, *refs)

    def place_of(k):
        return sum(jnp.where(k == i, max(place, 1) - 1, 0) for i, (place, _) in enumerate(steps))

    flat = pl.BlockSpec((rows, columns), lambda n, k, page_of, me: (0, n))
    operands = [p for group in pieces for p in group]
    in_specs = [pl.BlockSpec(p.shape, lambda n, k, page_of, me: (0, 0)) for p in operands]
    operands += [w_out, w_all]
    in_specs += [
        pl.BlockSpec((w_out.shape[0], columns), lambda n, k, page_of, me: (0, me[0] * cuts + n)),
        pl.BlockSpec(
            (outer, 1, 1, stored, columns),
            lambda n, k, page_of, me: (0, n, place_of(k), 0, 0),
        ),
    ]
    if before is not None:
        operands.append(before)
        in_specs.append(flat)
    if hidden is not None:
        operands.append(hidden)
        in_specs.append(
            pl.BlockSpec((rows // PAGE, PAGE, columns), lambda n, k, page_of, me: (0, 0, n))
        )
    return pl.pallas_call(
        kernel,
        out_shape=jax.ShapeDtypeStruct((rows, cuts * columns), jnp.float32),
        grid_spec=pltpu.PrefetchScalarGridSpec(
            num_scalar_prefetch=2,
            grid=(cuts, len(steps)),
            in_specs=in_specs,
            out_specs=flat,
        ),
        compiler_params=pltpu.CompilerParams(vmem_limit_bytes=36 * MIB),
        cost_estimate=SMALL,
        name="mix_near",
    )(page_of, me, *operands)


def mix_far_kernel(blocks, cut, page_of, top, low, w_all, before, out):
    step = pl.program_id(1)
    band = rows_of(w_all, cut)

    def finish(piece):
        rows = before[...] + jnp.dot(piece[...], band, preferred_element_type=jnp.float32)
        rows = rows.astype(jnp.bfloat16)
        count = rows.shape[0] // PAGE
        for item in range(count):
            out[page_of[step * count + item]] = rows[item * PAGE : (item + 1) * PAGE]

    pl.when(step < blocks // 2)(lambda: finish(top))
    pl.when(step >= blocks // 2)(lambda: finish(low))


def mix_far(page_of, top, low, cut, w_all, before):
    blocks = 4
    half, width = top.shape
    outer, cuts, places, stored, columns = w_all.shape
    block = 2 * half // blocks
    pages = 2 * half // PAGE

    def kernel(*refs):
        mix_far_kernel(blocks, cut, *refs)

    return pl.pallas_call(
        kernel,
        out_shape=jax.ShapeDtypeStruct((pages, PAGE, cuts * columns), jnp.bfloat16),
        grid_spec=pltpu.PrefetchScalarGridSpec(
            num_scalar_prefetch=1,
            grid=(cuts, blocks),
            in_specs=[
                pl.BlockSpec((block, width), lambda n, r, page_of: (jnp.minimum(r, blocks // 2 - 1), 0)),
                pl.BlockSpec((block, width), lambda n, r, page_of: (jnp.maximum(r - blocks // 2, 0), 0)),
                pl.BlockSpec(
                    (outer, 1, 1, stored, columns), lambda n, r, page_of: (0, n, places - 1, 0, 0)
                ),
                pl.BlockSpec((block, columns), lambda n, r, page_of: (r, n)),
            ],
            out_specs=pl.BlockSpec((pages, PAGE, columns), lambda n, r, page_of: (0, 0, n)),
        ),
        compiler_params=pltpu.CompilerParams(vmem_limit_bytes=20 * MIB),
        cost_estimate=SMALL,
        name="mix_far",
    )(page_of, top, low, w_all, before)


def w_out_shares(w_out, context, outer_index, outer, cuts):
    columns = w_out.shape[1] // (2 * TENSOR)
    bands = []
    for first, end in cuts:
        depth = (end - first) * HEAD // outer
        bands.append(
            lax.dynamic_slice_in_dim(w_out, first * HEAD + outer_index * depth, depth, 0)
        )
    band = jnp.concatenate(bands, axis=0)
    me = lax.axis_index("tensor")
    right, far, left = [
        lax.dynamic_slice_in_dim(band, ((me + step) % TENSOR * 2 + context) * columns, columns, 1)
        for step in range(1, TENSOR)
    ]
    far = lax.ppermute(far, "tensor", [(i, (i + 2) % TENSOR) for i in range(TENSOR)])
    return [to_right(right), to_left(left), far]


def places(local, sequence):
    pages = local.shape[0]
    ladder = jnp.arange(pages, dtype=jnp.int32)
    hit = local[None, :] == ladder[:, None]
    source = jnp.sum(jnp.where(hit, ladder[None, :], 0), axis=1)
    return jnp.stack([source, jnp.sum(jnp.where(hit, sequence[None, :], 0), axis=1)])


def read_facts(facts):
    facts = facts.astype(jnp.float32).astype(jnp.int32)
    return places(facts[:, 0], facts[:, 1] * DIGIT + facts[:, 2])


def body(hidden, seq_id, dest_page, norm_gain, w_query, q_bias, w_key, w_value, v_bias, w_out):
    pages = dest_page.shape[0]
    me = lax.axis_index("tensor")
    context = lax.axis_index("context")
    heads = w_query.shape[1] // HEAD
    cuts = [(0, 3), (3, heads)]
    order = jnp.stack([me, (me + 3) % TENSOR, (me + 1) % TENSOR, (me + 2) % TENSOR]).astype(jnp.int32)
    sequence = seq_id[::PAGE]
    group = dest_page // pages
    page = jnp.concatenate([group, dest_page % pages, sequence // DIGIT, sequence % DIGIT])
    slots = jnp.arange(pages, dtype=jnp.int32)
    page_of = jnp.sum(jnp.where(group[None, :] == slots[:, None], slots[None, :], 0), axis=1)

    paged = hidden.reshape(pages, PAGE, hidden.shape[1])
    block = jnp.split(hidden, 2)
    w_query, w_key, w_value, block = lax.optimization_barrier((w_query, w_key, w_value, block))
    width, heads_wide = hidden.shape[1], w_query.shape[1]

    def band(array, index):
        return lax.dynamic_slice_in_dim(array, order[index] * width, width, 0)

    weights = [
        jnp.concatenate([band(w, index) for w in (w_query, w_key, w_value)], axis=1)
        for index in range(TENSOR)
    ]
    gains = [band(norm_gain, index)[None, :] for index in range(TENSOR)]
    near_gains, far_gain = jnp.stack(gains[:3]), gains[3][None]
    bias = jnp.concatenate([q_bias, jnp.zeros_like(v_bias), v_bias]).astype(jnp.float32)[None, :]
    hold = lax.optimization_barrier

    def exchange(rows):
        return lax.all_to_all(rows, DP, split_axis=0, concat_axis=0, tiled=True)

    left, right = ring_near(*block)
    shares = w_out_shares(w_out, context, lax.axis_index(("z", "xh")), 8, cuts)
    shares, _ = hold((shares, (left[0], right[1])))
    w_all = lax.all_gather(jnp.stack(shares), ("z", "xh", "context"), axis=0, tiled=False)
    w_all = w_all.reshape((8, 2) + w_all.shape[1:])
    left, right, weights, near_gains = hold((left, right, weights, near_gains))
    far = ring_far(left[0], right[1])
    carry = project_near((block, left, right), weights[:3], near_gains)
    queries, own = project_far(page, *far, weights[3], far_gain, bias, carry, heads_wide)
    own = exchange(own)
    queries, own = hold((queries, own))
    queries = exchange(queries)
    other = lax.ppermute(own, "context", [(0, 1)])

    here = read_facts(own[:, 0, 2 * HEAD : 2 * HEAD + 3])
    there = read_facts(other[:, 0, 2 * HEAD : 2 * HEAD + 3])
    there = jnp.where(context > 0, there, here)
    source = jnp.concatenate([there[0], here[0]])
    sequence = jnp.concatenate([there[1], here[1]])

    second = context.astype(jnp.int32).reshape(1)
    (first, end), (start, stop) = cuts
    part_a = attend(end - first, first, source, sequence, second, queries, own, other)
    queries, part_a = hold((queries, part_a))
    part_b = attend(stop - start, start, source, sequence, second, queries, own, other)
    part_a, part_b = hold((exchange(part_a), part_b))
    flat_a = part_a.reshape(pages * PAGE, -1)
    left, right = to_right(flat_a), to_left(flat_a)
    flat_b = exchange(part_b).reshape(pages * PAGE, -1)
    left, right, flat_b = hold((left, right, flat_b))
    bands = [(first * HEAD // 8, end * HEAD // 8) for first, end in cuts]
    here = me.astype(jnp.int32).reshape(1)
    half = pages * PAGE // 2
    far = ring_far(left[:half], right[half:])
    steps = [(0, bands[0]), (1, bands[0]), (2, bands[0]), (0, bands[1])]
    pieces = [(flat_a,), (left,), (right,), (flat_b,)]
    total = mix_near(page_of, here, pieces, steps, w_out, w_all)
    left, right = to_right(flat_b), to_left(flat_b)
    left, right, far, total = hold((left, right, far, total))
    last = ring_far(left[:half], right[half:])
    steps = [(3, bands[0]), (1, bands[1]), (2, bands[1])]
    total = mix_near(page_of, here, [far, (left,), (right,)], steps, w_out, w_all, total, paged)
    result = mix_far(page_of, *last, bands[1], w_all, total)
    return result.reshape(hidden.shape)


def solution(mesh):
    fine = Mesh(
        mesh.devices.reshape(4, 2, 2, 2, TENSOR), ("z", "xh", "core", "context", "tensor")
    )
    rows = DP + ("context",)
    return jax.shard_map(
        body,
        mesh=fine,
        in_specs=(
            P(rows, "tensor"),
            P(rows),
            P(rows),
            P(),
            P(None, "tensor"),
            P("tensor"),
            P(None, "tensor"),
            P(None, "tensor"),
            P("tensor"),
            P("tensor", None),
        ),
        out_specs=P(rows, "tensor"),
        check_vma=False,
    )
```

```python
import math

import jax
import jax.numpy as jnp
from jax import lax
from jax.experimental import pallas as pl
from jax.experimental.pallas import tpu as pltpu
from jax.sharding import Mesh
from jax.sharding import PartitionSpec as P

HEAD = 128
PAGE = 64
EPSILON = 1e-06
DP = ("z", "xh", "core")
TENSOR = 4
RING = 4
X = ("xh", "context")
MIB = 1024 * 1024
SMALL = pl.CostEstimate(flops=1024, bytes_accessed=1024, transcendentals=0)


def to_right(block, axis="tensor"):
    return lax.ppermute(block, axis, [(i, (i + 1) % RING) for i in range(RING)])


def to_left(block, axis="tensor"):
    return lax.ppermute(block, axis, [(i, (i - 1) % RING) for i in range(RING)])


def ring_near(top, low):
    return (to_right(top), to_right(low)), (to_left(top), to_left(low))


def ring_far(left, right):
    return to_right(left), to_left(right)


def project_near_kernel(count, *refs):
    pieces, weights, gains = refs[: 2 * count], refs[2 * count : 3 * count], refs[3 * count]
    total, squares = refs[3 * count + 1 :]
    step = pl.program_id(0)
    for index in range(count):

        @pl.when(step == index)
        def _(index=index):
            for half in range(2):
                piece = pieces[2 * index + half]
                at = pl.ds(half * piece.shape[0], piece.shape[0])
                product, square = banded(piece, gains[index], weights[index])
                if index == 0:
                    total[at], squares[at] = product, square
                else:
                    total[at], squares[at] = total[at] + product, squares[at] + square


def banded(piece, gain, weights):
    wide = piece[...].astype(jnp.float32)
    scaled = (wide * gain.astype(jnp.float32)).astype(jnp.bfloat16)
    product = jnp.dot(scaled, weights[...], preferred_element_type=jnp.float32)
    return product, jnp.sum(wide * wide, axis=1, keepdims=True)


def project_near(pieces, weights, gains):
    count = len(pieces)
    half, width = pieces[0][0].shape
    rows = 2 * half
    pieces = [half for piece in pieces for half in piece]
    columns = weights[0].shape[1]
    sums = [(rows, columns), (rows, 1)]

    def kernel(*refs):
        project_near_kernel(count, *refs)

    def whole(shape):
        return pl.BlockSpec(shape, lambda k: (0,) * len(shape))

    return pl.pallas_call(
        kernel,
        out_shape=[jax.ShapeDtypeStruct(shape, jnp.float32) for shape in sums],
        grid=(count,),
        in_specs=[whole((half, width)) for _ in pieces]
        + [whole(a.shape) for a in (*weights, gains)],
        out_specs=[whole(shape) for shape in sums],
        compiler_params=pltpu.CompilerParams(vmem_limit_bytes=56 * MIB),
        cost_estimate=SMALL,
        name="project_near",
    )(*pieces, *weights, gains)


def project_far_kernel(blocks, group, top, low, weights, gain, bias, total, squares, *outs):
    step = pl.program_id(0)
    pages, count, _ = outs[0].shape
    features = TENSOR * top.shape[1]

    def finish(piece):
        product, square = banded(piece, gain[0], weights)
        scale = lax.rsqrt((squares[...] + square) * (1.0 / features) + EPSILON)
        result = ((total[...] + product) * scale + bias[...]).astype(jnp.bfloat16)
        for item in range(pages // blocks):
            target = group[step * (pages // blocks) + item]
            rows = result[item * count : (item + 1) * count]
            at = 0
            for out in outs:
                out[target] = rows[:, at : at + out.shape[2]]
                at += out.shape[2]

    pl.when(step < blocks // 2)(lambda: finish(top))
    pl.when(step >= blocks // 2)(lambda: finish(low))


def project_far(group, top, low, weights, gain, bias, carry, split):
    blocks = 4
    half, width = carry[0].shape[0] // 2, top.shape[1]
    columns = weights.shape[1]
    pages = group.shape[0]
    block = 2 * half // blocks
    shapes = [(pages, 2 * half // pages, wide) for wide in (split, columns - split)]

    def kernel(*refs):
        project_far_kernel(blocks, *refs)

    def whole(shape):
        return pl.BlockSpec(shape, lambda r, group: (0,) * len(shape))

    return pl.pallas_call(
        kernel,
        out_shape=[jax.ShapeDtypeStruct(shape, jnp.bfloat16) for shape in shapes],
        grid_spec=pltpu.PrefetchScalarGridSpec(
            num_scalar_prefetch=1,
            grid=(blocks,),
            in_specs=[
                pl.BlockSpec((block, width), lambda r, group: (jnp.minimum(r, blocks // 2 - 1), 0)),
                pl.BlockSpec((block, width), lambda r, group: (jnp.maximum(r - blocks // 2, 0), 0)),
                whole(weights.shape),
                whole(gain.shape),
                whole(bias.shape),
                pl.BlockSpec((block, columns), lambda r, group: (r, 0)),
                pl.BlockSpec((block, 1), lambda r, group: (r, 0)),
            ],
            out_specs=[whole(shape) for shape in shapes],
        ),
        compiler_params=pltpu.CompilerParams(vmem_limit_bytes=28 * MIB),
        cost_estimate=SMALL,
        name="project_far",
    )(group, top, low, weights, gain, bias, *carry)


def attend_kernel(heads, first, source, sequence, context, queries, own, other, out, *scratch):
    keys, values, turned, best, total, summed = scratch
    pages = own.shape[0]
    half = pages * PAGE
    per = 4
    rows = per * PAGE
    blocks = pages // per
    lanes = heads * rows
    factor = math.log2(math.e) / math.sqrt(HEAD)

    def place_page(slot, carry):
        for base, lookup, array in ((0, 0, other), (half, pages, own)):
            page = source[lookup + slot]
            at = pl.ds(pl.multiple_of(base + slot * PAGE, PAGE), PAGE)
            keys[at, :] = array[page, :, :HEAD]
            values[at, :] = array[page, :, HEAD : 2 * HEAD]
        return carry

    lax.fori_loop(0, pages, place_page, 0)
    for block in range(2 * blocks):
        turned[block] = values[pl.ds(block * rows, rows), :].astype(jnp.float32).T.astype(jnp.bfloat16)

    def query_block(index, carry):
        slot = index * per
        query = jnp.concatenate(
            [
                queries[source[pages + slot + page], :, first + head * HEAD : first + (head + 1) * HEAD]
                for head in range(heads)
                for page in range(per)
            ],
            axis=0,
        )
        sequence_q = [sequence[pages + slot + page] for page in range(per)]
        within = lax.broadcasted_iota(jnp.int32, (1, lanes), 1) % rows
        seq_lane = jnp.full((1, lanes), sequence_q[per - 1], jnp.int32)
        for page in range(per - 2, -1, -1):
            seq_lane = jnp.where(within < (page + 1) * PAGE, sequence_q[page], seq_lane)

        def scores_of(block, diagonal):
            at = pl.ds(pl.multiple_of(block * rows, rows), rows)
            scores = lax.dot_general(
                keys[at, :], query, (((1,), (1,)), ((), ())), preferred_element_type=jnp.float32
            )
            cut = []
            for page in range(per):
                visible = seq_lane == sequence[block * per + page]
                if diagonal:
                    place = lax.broadcasted_iota(jnp.int32, (PAGE, lanes), 0) + page * PAGE
                    visible = visible & (place <= within)
                cut.append(jnp.where(visible, scores[page * PAGE : (page + 1) * PAGE], -1e30))
            return jnp.concatenate(cut, axis=0)

        def apply(block, weight):
            return jnp.dot(
                turned[block], weight.astype(jnp.bfloat16), preferred_element_type=jnp.float32
            )

        last = blocks + index
        scores = scores_of(last, True)
        top = jnp.max(scores, axis=0, keepdims=True)
        weight = jnp.exp2((scores - top) * factor)
        best[...] = top
        total[...] = jnp.sum(weight, axis=0, keepdims=True)
        summed[...] = apply(last, weight)

        def key_block(block, carry):
            seen = False
            for page in range(per):
                for seq in sequence_q:
                    seen = seen | (sequence[block * per + page] == seq)

            @pl.when(seen)
            def _():
                scores = scores_of(block, False)
                top = jnp.maximum(best[...], jnp.max(scores, axis=0, keepdims=True))
                weight = jnp.exp2((scores - top) * factor)
                fade = jnp.exp2((best[...] - top) * factor)
                best[...] = top
                total[...] = total[...] * fade + jnp.sum(weight, axis=0, keepdims=True)
                summed[...] = summed[...] * fade + apply(block, weight)

            return carry

        lax.fori_loop(jnp.where(context[0] > 0, 0, blocks), last, key_block, 0)
        result = (summed[...] / total[...]).T.astype(jnp.bfloat16)
        for head in range(heads):
            for page in range(per):
                start = head * rows + page * PAGE
                out[source[pages + slot + page], :, head * HEAD : (head + 1) * HEAD] = result[
                    start : start + PAGE
                ]
        return carry

    lax.fori_loop(0, blocks, query_block, 0)


def attend(heads, first, source, sequence, context, queries, own, other):
    pages = own.shape[0]

    def kernel(*refs):
        attend_kernel(heads, first, *refs)

    half = pages * PAGE
    lanes = heads * 4 * PAGE
    vmem = pl.BlockSpec(memory_space=pltpu.VMEM)
    smem = pl.BlockSpec(memory_space=pltpu.SMEM)
    return pl.pallas_call(
        kernel,
        out_shape=jax.ShapeDtypeStruct((pages, PAGE, heads * HEAD), jnp.bfloat16),
        in_specs=[smem] * 3 + [vmem] * 3,
        out_specs=vmem,
        scratch_shapes=[
            pltpu.VMEM((2 * half, HEAD), jnp.bfloat16),
            pltpu.VMEM((2 * half, HEAD), jnp.bfloat16),
            pltpu.VMEM((pages // 2, HEAD, 4 * PAGE), jnp.bfloat16),
            pltpu.VMEM((1, lanes), jnp.float32),
            pltpu.VMEM((1, lanes), jnp.float32),
            pltpu.VMEM((HEAD, lanes), jnp.float32),
        ],
        compiler_params=pltpu.CompilerParams(vmem_limit_bytes=20 * MIB),
        cost_estimate=SMALL,
        name="attend",
    )(source, sequence, context, queries, own, other)


def rows_of(w_out, place, cut):
    begin, end = cut
    return w_out[:, 0, place, begin:end, :].reshape(-1, w_out.shape[-1])


def mix_near_kernel(steps, counts, carried, paged, page_of, me, *refs):
    refs = list(refs)
    pieces = [[refs.pop(0) for _ in range(count)] for count in counts]
    w_own, w_all = refs.pop(0), refs.pop(0)
    before = refs.pop(0) if carried else None
    hidden = refs.pop(0) if paged else None
    (total,) = refs
    block = pl.program_id(1)
    bands = [
        w_own[8 * cut[0] : 8 * cut[1], :] if place == 0 else rows_of(w_all, place - 1, cut)
        for place, cut in steps
    ]
    band = jnp.concatenate(bands, axis=0)

    def finish(half):
        rows = jnp.concatenate([piece[min(half, len(piece) - 1)][...] for piece in pieces], axis=1)
        product = jnp.dot(rows, band, preferred_element_type=jnp.float32)
        if carried:
            product = before[...] + product
        if paged:
            count = rows.shape[0] // PAGE
            added = [hidden[page_of[half * count + item]] for item in range(count)]
            product = product + jnp.concatenate(added, axis=0).astype(jnp.float32)
        total[...] = product

    for half in range(2):
        pl.when(block == half)(lambda half=half: finish(half))


def mix_near(page_of, me, pieces, steps, w_out, w_all, before=None, hidden=None):
    outer, cuts, places, stored, columns = w_all.shape
    counts = [len(piece) for piece in pieces]
    half = sum(p.shape[0] for p in pieces[0]) // 2

    def kernel(*refs):
        mix_near_kernel(steps, counts, before is not None, hidden is not None, *refs)

    flat = pl.BlockSpec((half, columns), lambda n, r, page_of, me: (r, n))
    operands, in_specs = [], []
    for piece in pieces:
        for array in piece:
            operands.append(array)
            whole = len(piece) > 1
            in_specs.append(
                pl.BlockSpec(
                    (half, array.shape[1]),
                    lambda n, r, page_of, me, whole=whole: (0 if whole else r, 0),
                )
            )
    operands += [w_out, w_all]
    in_specs += [
        pl.BlockSpec((w_out.shape[0], columns), lambda n, r, page_of, me: (0, me[0] * cuts + n)),
        pl.BlockSpec(
            (outer, 1, places, stored, columns), lambda n, r, page_of, me: (0, n, 0, 0, 0)
        ),
    ]
    if before is not None:
        operands.append(before)
        in_specs.append(flat)
    if hidden is not None:
        operands.append(hidden)
        in_specs.append(
            pl.BlockSpec((2 * half // PAGE, PAGE, columns), lambda n, r, page_of, me: (0, 0, n))
        )
    return pl.pallas_call(
        kernel,
        out_shape=jax.ShapeDtypeStruct((2 * half, cuts * columns), jnp.float32),
        grid_spec=pltpu.PrefetchScalarGridSpec(
            num_scalar_prefetch=2,
            grid=(cuts, 2),
            in_specs=in_specs,
            out_specs=flat,
        ),
        compiler_params=pltpu.CompilerParams(vmem_limit_bytes=36 * MIB),
        cost_estimate=SMALL,
        name="mix_near",
    )(page_of, me, *operands)


def mix_far_kernel(blocks, cut, page_of, top, low, w_all, before, out):
    step = pl.program_id(1)
    band = rows_of(w_all, 0, cut)

    def finish(piece):
        rows = before[...] + jnp.dot(piece[...], band, preferred_element_type=jnp.float32)
        rows = rows.astype(jnp.bfloat16)
        count = rows.shape[0] // PAGE
        for item in range(count):
            out[page_of[step * count + item]] = rows[item * PAGE : (item + 1) * PAGE]

    pl.when(step < blocks // 2)(lambda: finish(top))
    pl.when(step >= blocks // 2)(lambda: finish(low))


def mix_far(page_of, top, low, cut, w_all, before):
    blocks = 4
    half, width = top.shape
    outer, cuts, places, stored, columns = w_all.shape
    block = 2 * half // blocks
    pages = 2 * half // PAGE

    def kernel(*refs):
        mix_far_kernel(blocks, cut, *refs)

    return pl.pallas_call(
        kernel,
        out_shape=jax.ShapeDtypeStruct((pages, PAGE, cuts * columns), jnp.bfloat16),
        grid_spec=pltpu.PrefetchScalarGridSpec(
            num_scalar_prefetch=1,
            grid=(cuts, blocks),
            in_specs=[
                pl.BlockSpec((block, width), lambda n, r, page_of: (jnp.minimum(r, blocks // 2 - 1), 0)),
                pl.BlockSpec((block, width), lambda n, r, page_of: (jnp.maximum(r - blocks // 2, 0), 0)),
                pl.BlockSpec(
                    (outer, 1, 1, stored, columns), lambda n, r, page_of: (0, n, places - 1, 0, 0)
                ),
                pl.BlockSpec((block, columns), lambda n, r, page_of: (r, n)),
            ],
            out_specs=pl.BlockSpec((pages, PAGE, columns), lambda n, r, page_of: (0, 0, n)),
        ),
        compiler_params=pltpu.CompilerParams(vmem_limit_bytes=20 * MIB),
        cost_estimate=SMALL,
        name="mix_far",
    )(page_of, top, low, w_all, before)


def w_out_shares(w_out, context, outer_index, outer, cuts):
    columns = w_out.shape[1] // (2 * TENSOR)
    bands = []
    for first, end in cuts:
        depth = (end - first) * HEAD // outer
        bands.append(
            lax.dynamic_slice_in_dim(w_out, first * HEAD + outer_index * depth, depth, 0)
        )
    band = jnp.concatenate(bands, axis=0)
    me = lax.axis_index("tensor")
    right, far, left = [
        lax.dynamic_slice_in_dim(band, ((me + step) % TENSOR * 2 + context) * columns, columns, 1)
        for step in range(1, TENSOR)
    ]
    far = lax.ppermute(far, "tensor", [(i, (i + 2) % TENSOR) for i in range(TENSOR)])
    return [to_right(right), to_left(left), far]


def place_kernel(where, *refs):
    sources, out = refs[:-1], refs[-1]
    every = (0, 3, 1, 2)
    for z_step, x_steps, source in zip((*every, 2), (every, every, every, every[:2], every[2:]), sources):
        z = lax.rem(where[0] + z_step, RING)
        for index, x_step in enumerate(x_steps):
            x = lax.rem(where[1] + x_step, RING)
            out[z * 2 + x // 2, lax.rem(x, 2)] = source[index]


def place_shares(sources):
    where = jnp.stack([lax.axis_index("z"), lax.axis_index(X)]).astype(jnp.int32)
    vmem = pl.BlockSpec(memory_space=pltpu.VMEM)
    return pl.pallas_call(
        place_kernel,
        out_shape=jax.ShapeDtypeStruct((8, 2) + sources[0].shape[1:], jnp.bfloat16),
        in_specs=[pl.BlockSpec(memory_space=pltpu.SMEM)] + [vmem] * len(sources),
        out_specs=vmem,
        compiler_params=pltpu.CompilerParams(vmem_limit_bytes=24 * MIB),
        cost_estimate=SMALL,
        name="place_shares",
    )(where, *sources)


def places(local, sequence):
    pages = local.shape[0]
    ladder = jnp.arange(pages, dtype=jnp.int32)
    hit = local[None, :] == ladder[:, None]
    source = jnp.sum(jnp.where(hit, ladder[None, :], 0), axis=1)
    return jnp.stack([source, jnp.sum(jnp.where(hit, sequence[None, :], 0), axis=1)])


def body(hidden, seq_id, dest_page, norm_gain, w_query, q_bias, w_key, w_value, v_bias, w_out):
    pages = dest_page.shape[0]
    me = lax.axis_index("tensor")
    context = lax.axis_index("context")
    heads = w_query.shape[1] // HEAD
    cuts = [(0, 3), (3, heads)]
    order = jnp.stack([me, (me + 3) % TENSOR, (me + 1) % TENSOR, (me + 2) % TENSOR]).astype(jnp.int32)
    sequence = seq_id[::PAGE]
    group = dest_page // pages
    slots = jnp.arange(pages, dtype=jnp.int32)
    page_of = jnp.sum(jnp.where(group[None, :] == slots[:, None], slots[None, :], 0), axis=1)

    paged = hidden.reshape(pages, PAGE, hidden.shape[1])
    block = jnp.split(hidden, 2)
    width = hidden.shape[1]

    def band(array, index):
        return lax.dynamic_slice_in_dim(array, order[index] * width, width, 0)

    hold = lax.optimization_barrier

    def exchange(rows):
        return lax.all_to_all(rows, DP, split_axis=0, concat_axis=0, tiled=True)

    def beside(rows):
        return lax.ppermute(rows, "context", [(0, 1)])

    shares = w_out_shares(w_out, context, lax.axis_index(("z", "xh")), 8, cuts)
    block, shares = hold((block, shares))
    left, right = ring_near(*block)
    shares = jnp.stack(shares)
    x_left, x_right = to_right(shares, X), to_left(shares, X)
    depth = (cuts[0][1] - cuts[0][0]) * HEAD // 8
    x_top, x_low = to_right(x_left[:, :depth], X), to_left(x_right[:, depth:], X)
    shares = jnp.stack([shares, x_left, x_right, jnp.concatenate([x_top, x_low], axis=1)])

    w_query, w_key, w_value, block = hold((w_query, w_key, w_value, block))
    weights = [
        jnp.concatenate([band(w, index) for w in (w_key, w_value, w_query)], axis=1)
        for index in range(TENSOR)
    ]
    gains = [band(norm_gain, index)[None, :] for index in range(TENSOR)]
    near_gains, far_gain = jnp.stack(gains[:3]), gains[3][None]
    bias = jnp.concatenate([jnp.zeros_like(v_bias), v_bias, q_bias]).astype(jnp.float32)[None, :]

    facts = jnp.stack([jnp.take(dest_page % pages, page_of), jnp.take(sequence, page_of)], axis=1)
    facts, _ = hold((facts, block))
    facts = exchange(facts)
    facts = jnp.stack([facts, beside(facts)])
    here = places(facts[0, :, 0], facts[0, :, 1])
    there = jnp.where(context > 0, places(facts[1, :, 0], facts[1, :, 1]), here)
    source = jnp.concatenate([there[0], here[0]])
    sequence = jnp.concatenate([there[1], here[1]])

    top, low, weights, near_gains, source, sequence, shares = hold(
        (left[0], right[1], weights, near_gains, source, sequence, shares)
    )
    far = ring_far(top, low)
    z_left, z_right = to_right(shares, "z"), to_left(shares, "z")
    left, right, z_left, z_right = hold((left, right, z_left, z_right))
    z_far = (to_right(z_left[:2], "z"), to_left(z_right[2:], "z"))
    carry = project_near((block, left, right), weights[:3], near_gains)
    (first, end), (start, stop) = cuts
    split = (2 + end) * HEAD
    far, z_far = hold((far, z_far))
    w_all = place_shares([shares, z_left, z_right, *z_far])
    own, queries = project_far(group, *far, weights[3], far_gain, bias, carry, split)
    own = exchange(own)
    other = beside(own[:, :, : 2 * HEAD])
    queries, own = hold((queries, own))
    queries = exchange(queries)

    second = context.astype(jnp.int32).reshape(1)
    own, w_all = hold((own, w_all))
    part_a = attend(end - first, 2 * HEAD, source, sequence, second, own, own, other)
    own, part_a = hold((own, part_a))
    part_b = attend(stop - start, 0, source, sequence, second, queries, own, other)
    part_a, part_b = hold((exchange(part_a), part_b))
    flat_a = part_a.reshape(pages * PAGE, -1)
    left, right = to_right(flat_a), to_left(flat_a)
    flat_b = exchange(part_b).reshape(pages * PAGE, -1)
    left, right, flat_b = hold((left, right, flat_b))
    bands = [(first * HEAD // 8, end * HEAD // 8) for first, end in cuts]
    here = me.astype(jnp.int32).reshape(1)
    half = pages * PAGE // 2
    far = ring_far(left[:half], right[half:])
    steps = [(0, bands[0]), (1, bands[0]), (2, bands[0]), (0, bands[1])]
    pieces = [(flat_a,), (left,), (right,), (flat_b,)]
    total = mix_near(page_of, here, pieces, steps, w_out, w_all)
    left, right = to_right(flat_b), to_left(flat_b)
    left, right, far, total = hold((left, right, far, total))
    last = ring_far(left[:half], right[half:])
    steps = [(3, bands[0]), (1, bands[1]), (2, bands[1])]
    total = mix_near(page_of, here, [far, (left,), (right,)], steps, w_out, w_all, total, paged)
    result = mix_far(page_of, *last, bands[1], w_all, total)
    return result.reshape(hidden.shape)


def solution(mesh):
    fine = Mesh(
        mesh.devices.reshape(4, 2, 2, 2, TENSOR), ("z", "xh", "core", "context", "tensor")
    )
    rows = DP + ("context",)
    return jax.shard_map(
        body,
        mesh=fine,
        in_specs=(
            P(rows, "tensor"),
            P(rows),
            P(rows),
            P(),
            P(None, "tensor"),
            P("tensor"),
            P(None, "tensor"),
            P(None, "tensor"),
            P("tensor"),
            P("tensor", None),
        ),
        out_specs=P(rows, "tensor"),
        check_vma=False,
    )
```

```python
import math

import jax
import jax.numpy as jnp
from jax import lax
from jax.experimental import pallas as pl
from jax.experimental.pallas import tpu as pltpu
from jax.sharding import Mesh
from jax.sharding import PartitionSpec as P

HEAD = 128
PAGE = 64
EPSILON = 1e-06
DP = ("z", "xh", "core")
TENSOR = 4
RING = 4
X = ("xh", "context")
MIB = 1024 * 1024
SMALL = pl.CostEstimate(flops=1024, bytes_accessed=1024, transcendentals=0)


def to_right(block, axis="tensor"):
    return lax.ppermute(block, axis, [(i, (i + 1) % RING) for i in range(RING)])


def to_left(block, axis="tensor"):
    return lax.ppermute(block, axis, [(i, (i - 1) % RING) for i in range(RING)])


def ring_near(top, low):
    return (to_right(top), to_right(low)), (to_left(top), to_left(low))


def ring_far(left, right):
    return to_right(left), to_left(right)


def project_near_kernel(count, *refs):
    pieces, weights, gains = refs[: 2 * count], refs[2 * count : 3 * count], refs[3 * count]
    total, squares = refs[3 * count + 1 :]
    step = pl.program_id(0)
    for index in range(count):

        @pl.when(step == index)
        def _(index=index):
            for half in range(2):
                piece = pieces[2 * index + half]
                at = pl.ds(half * piece.shape[0], piece.shape[0])
                product, square = banded(piece, gains[index], weights[index])
                if index == 0:
                    total[at], squares[at] = product, square
                else:
                    total[at], squares[at] = total[at] + product, squares[at] + square


def banded(piece, gain, weights):
    wide = piece[...].astype(jnp.float32)
    scaled = (wide * gain.astype(jnp.float32)).astype(jnp.bfloat16)
    product = jnp.dot(scaled, weights[...], preferred_element_type=jnp.float32)
    return product, jnp.sum(wide * wide, axis=1, keepdims=True)


def project_near(pieces, weights, gains):
    count = len(pieces)
    half, width = pieces[0][0].shape
    rows = 2 * half
    pieces = [half for piece in pieces for half in piece]
    columns = weights[0].shape[1]
    sums = [(rows, columns), (rows, 1)]

    def kernel(*refs):
        project_near_kernel(count, *refs)

    def whole(shape):
        return pl.BlockSpec(shape, lambda k: (0,) * len(shape))

    return pl.pallas_call(
        kernel,
        out_shape=[jax.ShapeDtypeStruct(shape, jnp.float32) for shape in sums],
        grid=(count,),
        in_specs=[whole((half, width)) for _ in pieces]
        + [whole(a.shape) for a in (*weights, gains)],
        out_specs=[whole(shape) for shape in sums],
        compiler_params=pltpu.CompilerParams(vmem_limit_bytes=56 * MIB),
        cost_estimate=SMALL,
        name="project_near",
    )(*pieces, *weights, gains)


def project_far_kernel(blocks, group, top, low, weights, gain, bias, total, squares, *outs):
    step = pl.program_id(0)
    pages, count, _ = outs[0].shape
    features = TENSOR * top.shape[1]

    def finish(piece):
        product, square = banded(piece, gain[0], weights)
        scale = lax.rsqrt((squares[...] + square) * (1.0 / features) + EPSILON)
        result = ((total[...] + product) * scale + bias[...]).astype(jnp.bfloat16)
        for item in range(pages // blocks):
            target = group[step * (pages // blocks) + item]
            rows = result[item * count : (item + 1) * count]
            at = 0
            for out in outs:
                out[target] = rows[:, at : at + out.shape[2]]
                at += out.shape[2]

    pl.when(step < blocks // 2)(lambda: finish(top))
    pl.when(step >= blocks // 2)(lambda: finish(low))


def project_far(group, top, low, weights, gain, bias, carry, split):
    blocks = 4
    half, width = carry[0].shape[0] // 2, top.shape[1]
    columns = weights.shape[1]
    pages = group.shape[0]
    block = 2 * half // blocks
    shapes = [(pages, 2 * half // pages, wide) for wide in (split, columns - split)]

    def kernel(*refs):
        project_far_kernel(blocks, *refs)

    def whole(shape):
        return pl.BlockSpec(shape, lambda r, group: (0,) * len(shape))

    return pl.pallas_call(
        kernel,
        out_shape=[jax.ShapeDtypeStruct(shape, jnp.bfloat16) for shape in shapes],
        grid_spec=pltpu.PrefetchScalarGridSpec(
            num_scalar_prefetch=1,
            grid=(blocks,),
            in_specs=[
                pl.BlockSpec((block, width), lambda r, group: (jnp.minimum(r, blocks // 2 - 1), 0)),
                pl.BlockSpec((block, width), lambda r, group: (jnp.maximum(r - blocks // 2, 0), 0)),
                whole(weights.shape),
                whole(gain.shape),
                whole(bias.shape),
                pl.BlockSpec((block, columns), lambda r, group: (r, 0)),
                pl.BlockSpec((block, 1), lambda r, group: (r, 0)),
            ],
            out_specs=[whole(shape) for shape in shapes],
        ),
        compiler_params=pltpu.CompilerParams(vmem_limit_bytes=28 * MIB),
        cost_estimate=SMALL,
        name="project_far",
    )(group, top, low, weights, gain, bias, *carry)


def attend_kernel(heads, first, begins, ends, source, sequence, context, queries, own, *refs):
    refs = list(refs)
    other = refs.pop(0) if ends else None
    state_in = [] if begins else [refs.pop(0) for _ in range(3)]
    outs = [refs.pop(0) for _ in range(1 if ends else 3)]
    keys, values, turned, best, total, summed = refs
    pages = own.shape[0]
    half = pages * PAGE
    per = 4
    rows = per * PAGE
    blocks = pages // per
    lanes = heads * rows
    factor = math.log2(math.e) / math.sqrt(HEAD)

    def place_page(slot, carry):
        for base, lookup, array in [(0, 0, other)] * ends + [(half, pages, own)] * begins:
            page = source[lookup + slot]
            at = pl.ds(pl.multiple_of(base + slot * PAGE, PAGE), PAGE)
            keys[at, :] = array[page, :, :HEAD]
            values[at, :] = array[page, :, HEAD : 2 * HEAD]
        return carry

    lax.fori_loop(0, pages, place_page, 0)
    for block in range(0 if ends else blocks, 2 * blocks if begins else blocks):
        turned[block] = values[pl.ds(block * rows, rows), :].astype(jnp.float32).T.astype(jnp.bfloat16)

    def query_block(index, carry):
        slot = index * per
        query = jnp.concatenate(
            [
                queries[source[pages + slot + page], :, first + head * HEAD : first + (head + 1) * HEAD]
                for head in range(heads)
                for page in range(per)
            ],
            axis=0,
        )
        sequence_q = [sequence[pages + slot + page] for page in range(per)]
        within = lax.broadcasted_iota(jnp.int32, (1, lanes), 1) % rows
        seq_lane = jnp.full((1, lanes), sequence_q[per - 1], jnp.int32)
        for page in range(per - 2, -1, -1):
            seq_lane = jnp.where(within < (page + 1) * PAGE, sequence_q[page], seq_lane)

        def scores_of(block, diagonal):
            at = pl.ds(pl.multiple_of(block * rows, rows), rows)
            scores = lax.dot_general(
                keys[at, :], query, (((1,), (1,)), ((), ())), preferred_element_type=jnp.float32
            )
            cut = []
            for page in range(per):
                visible = seq_lane == sequence[block * per + page]
                if diagonal:
                    place = lax.broadcasted_iota(jnp.int32, (PAGE, lanes), 0) + page * PAGE
                    visible = visible & (place <= within)
                cut.append(jnp.where(visible, scores[page * PAGE : (page + 1) * PAGE], -1e30))
            return jnp.concatenate(cut, axis=0)

        def apply(block, weight):
            return jnp.dot(
                turned[block], weight.astype(jnp.bfloat16), preferred_element_type=jnp.float32
            )

        last = blocks + index
        if begins:
            scores = scores_of(last, True)
            top = jnp.max(scores, axis=0, keepdims=True)
            weight = jnp.exp2((scores - top) * factor)
            best[...] = top
            total[...] = jnp.sum(weight, axis=0, keepdims=True)
            summed[...] = apply(last, weight)
        else:
            for held, array in zip((best, total, summed), state_in):
                held[...] = array[index]

        def key_block(block, carry):
            seen = False
            for page in range(per):
                for seq in sequence_q:
                    seen = seen | (sequence[block * per + page] == seq)

            @pl.when(seen)
            def _():
                scores = scores_of(block, False)
                top = jnp.maximum(best[...], jnp.max(scores, axis=0, keepdims=True))
                weight = jnp.exp2((scores - top) * factor)
                fade = jnp.exp2((best[...] - top) * factor)
                best[...] = top
                total[...] = total[...] * fade + jnp.sum(weight, axis=0, keepdims=True)
                summed[...] = summed[...] * fade + apply(block, weight)

            return carry

        begin = jnp.where(context[0] > 0, 0, blocks) if ends else blocks
        lax.fori_loop(begin, last if begins else blocks, key_block, 0)
        if not ends:
            for held, array in zip((best, total, summed), outs):
                array[index] = held[...]
            return carry
        result = (summed[...] / total[...]).T.astype(jnp.bfloat16)
        for head in range(heads):
            for page in range(per):
                start = head * rows + page * PAGE
                outs[0][source[pages + slot + page], :, head * HEAD : (head + 1) * HEAD] = result[
                    start : start + PAGE
                ]
        return carry

    lax.fori_loop(0, blocks, query_block, 0)


def attend(heads, first, source, sequence, context, queries, own, other=None, state=None):
    pages = own.shape[0]
    begins, ends = state is None, other is not None

    def kernel(*refs):
        attend_kernel(heads, first, begins, ends, *refs)

    half = pages * PAGE
    lanes = heads * 4 * PAGE
    vmem = pl.BlockSpec(memory_space=pltpu.VMEM)
    smem = pl.BlockSpec(memory_space=pltpu.SMEM)
    operands = [queries, own] + ([other] if ends else []) + list(state or [])
    if ends:
        out_shape = [jax.ShapeDtypeStruct((pages, PAGE, heads * HEAD), jnp.bfloat16)]
    else:
        out_shape = [
            jax.ShapeDtypeStruct((pages // 4, rows, lanes), jnp.float32) for rows in (1, 1, HEAD)
        ]
    outs = pl.pallas_call(
        kernel,
        out_shape=out_shape,
        in_specs=[smem] * 3 + [vmem] * len(operands),
        out_specs=[vmem] * len(out_shape),
        scratch_shapes=[
            pltpu.VMEM((2 * half, HEAD), jnp.bfloat16),
            pltpu.VMEM((2 * half, HEAD), jnp.bfloat16),
            pltpu.VMEM((pages // 2, HEAD, 4 * PAGE), jnp.bfloat16),
            pltpu.VMEM((1, lanes), jnp.float32),
            pltpu.VMEM((1, lanes), jnp.float32),
            pltpu.VMEM((HEAD, lanes), jnp.float32),
        ],
        compiler_params=pltpu.CompilerParams(vmem_limit_bytes=20 * MIB),
        cost_estimate=SMALL,
        name="attend",
    )(source, sequence, context, *operands)
    return outs[0] if ends else outs


def rows_of(w_out, place, cut):
    begin, end = cut
    return w_out[:, 0, place, begin:end, :].reshape(-1, w_out.shape[-1])


def mix_near_kernel(steps, counts, carried, paged, page_of, me, *refs):
    refs = list(refs)
    pieces = [[refs.pop(0) for _ in range(count)] for count in counts]
    w_own, w_all = refs.pop(0), refs.pop(0)
    before = refs.pop(0) if carried else None
    hidden = refs.pop(0) if paged else None
    (total,) = refs
    block = pl.program_id(1)
    bands = [
        w_own[8 * cut[0] : 8 * cut[1], :] if place == 0 else rows_of(w_all, place - 1, cut)
        for place, cut in steps
    ]
    band = jnp.concatenate(bands, axis=0)

    def finish(half):
        rows = jnp.concatenate([piece[min(half, len(piece) - 1)][...] for piece in pieces], axis=1)
        product = jnp.dot(rows, band, preferred_element_type=jnp.float32)
        if carried:
            product = before[...] + product
        if paged:
            count = rows.shape[0] // PAGE
            added = [hidden[page_of[half * count + item]] for item in range(count)]
            product = product + jnp.concatenate(added, axis=0).astype(jnp.float32)
        total[...] = product

    for half in range(2):
        pl.when(block == half)(lambda half=half: finish(half))


def mix_near(page_of, me, pieces, steps, w_out, w_all, before=None, hidden=None):
    outer, cuts, places, stored, columns = w_all.shape
    counts = [len(piece) for piece in pieces]
    half = sum(p.shape[0] for p in pieces[0]) // 2

    def kernel(*refs):
        mix_near_kernel(steps, counts, before is not None, hidden is not None, *refs)

    flat = pl.BlockSpec((half, columns), lambda n, r, page_of, me: (r, n))
    operands, in_specs = [], []
    for piece in pieces:
        for array in piece:
            operands.append(array)
            whole = len(piece) > 1
            in_specs.append(
                pl.BlockSpec(
                    (half, array.shape[1]),
                    lambda n, r, page_of, me, whole=whole: (0 if whole else r, 0),
                )
            )
    operands += [w_out, w_all]
    in_specs += [
        pl.BlockSpec((w_out.shape[0], columns), lambda n, r, page_of, me: (0, me[0] * cuts + n)),
        pl.BlockSpec(
            (outer, 1, places, stored, columns), lambda n, r, page_of, me: (0, n, 0, 0, 0)
        ),
    ]
    if before is not None:
        operands.append(before)
        in_specs.append(flat)
    if hidden is not None:
        operands.append(hidden)
        in_specs.append(
            pl.BlockSpec((2 * half // PAGE, PAGE, columns), lambda n, r, page_of, me: (0, 0, n))
        )
    return pl.pallas_call(
        kernel,
        out_shape=jax.ShapeDtypeStruct((2 * half, cuts * columns), jnp.float32),
        grid_spec=pltpu.PrefetchScalarGridSpec(
            num_scalar_prefetch=2,
            grid=(cuts, 2),
            in_specs=in_specs,
            out_specs=flat,
        ),
        compiler_params=pltpu.CompilerParams(vmem_limit_bytes=36 * MIB),
        cost_estimate=SMALL,
        name="mix_near",
    )(page_of, me, *operands)


def mix_far_kernel(blocks, cut, page_of, top, low, w_all, before, out):
    step = pl.program_id(1)
    band = rows_of(w_all, 0, cut)

    def finish(piece):
        rows = before[...] + jnp.dot(piece[...], band, preferred_element_type=jnp.float32)
        rows = rows.astype(jnp.bfloat16)
        count = rows.shape[0] // PAGE
        for item in range(count):
            out[page_of[step * count + item]] = rows[item * PAGE : (item + 1) * PAGE]

    pl.when(step < blocks // 2)(lambda: finish(top))
    pl.when(step >= blocks // 2)(lambda: finish(low))


def mix_far(page_of, top, low, cut, w_all, before):
    blocks = 4
    half, width = top.shape
    outer, cuts, places, stored, columns = w_all.shape
    block = 2 * half // blocks
    pages = 2 * half // PAGE

    def kernel(*refs):
        mix_far_kernel(blocks, cut, *refs)

    return pl.pallas_call(
        kernel,
        out_shape=jax.ShapeDtypeStruct((pages, PAGE, cuts * columns), jnp.bfloat16),
        grid_spec=pltpu.PrefetchScalarGridSpec(
            num_scalar_prefetch=1,
            grid=(cuts, blocks),
            in_specs=[
                pl.BlockSpec((block, width), lambda n, r, page_of: (jnp.minimum(r, blocks // 2 - 1), 0)),
                pl.BlockSpec((block, width), lambda n, r, page_of: (jnp.maximum(r - blocks // 2, 0), 0)),
                pl.BlockSpec(
                    (outer, 1, 1, stored, columns), lambda n, r, page_of: (0, n, places - 1, 0, 0)
                ),
                pl.BlockSpec((block, columns), lambda n, r, page_of: (r, n)),
            ],
            out_specs=pl.BlockSpec((pages, PAGE, columns), lambda n, r, page_of: (0, 0, n)),
        ),
        compiler_params=pltpu.CompilerParams(vmem_limit_bytes=20 * MIB),
        cost_estimate=SMALL,
        name="mix_far",
    )(page_of, top, low, w_all, before)


def w_out_shares(w_out, context, outer_index, outer, cuts):
    columns = w_out.shape[1] // (2 * TENSOR)
    bands = []
    for first, end in cuts:
        depth = (end - first) * HEAD // outer
        bands.append(
            lax.dynamic_slice_in_dim(w_out, first * HEAD + outer_index * depth, depth, 0)
        )
    band = jnp.concatenate(bands, axis=0)
    me = lax.axis_index("tensor")
    right, far, left = [
        lax.dynamic_slice_in_dim(band, ((me + step) % TENSOR * 2 + context) * columns, columns, 1)
        for step in range(1, TENSOR)
    ]
    far = lax.ppermute(far, "tensor", [(i, (i + 2) % TENSOR) for i in range(TENSOR)])
    return [to_right(right), to_left(left), far]


def place_kernel(where, *refs):
    sources, out = refs[:-1], refs[-1]
    every = (0, 3, 1, 2)
    for z_step, x_steps, source in zip((*every, 2), (every, every, every, every[:2], every[2:]), sources):
        z = lax.rem(where[0] + z_step, RING)
        for index, x_step in enumerate(x_steps):
            x = lax.rem(where[1] + x_step, RING)
            out[z * 2 + x // 2, lax.rem(x, 2)] = source[index]


def place_shares(sources):
    where = jnp.stack([lax.axis_index("z"), lax.axis_index(X)]).astype(jnp.int32)
    vmem = pl.BlockSpec(memory_space=pltpu.VMEM)
    return pl.pallas_call(
        place_kernel,
        out_shape=jax.ShapeDtypeStruct((8, 2) + sources[0].shape[1:], jnp.bfloat16),
        in_specs=[pl.BlockSpec(memory_space=pltpu.SMEM)] + [vmem] * len(sources),
        out_specs=vmem,
        compiler_params=pltpu.CompilerParams(vmem_limit_bytes=24 * MIB),
        cost_estimate=SMALL,
        name="place_shares",
    )(where, *sources)


def places(local, sequence):
    pages = local.shape[0]
    ladder = jnp.arange(pages, dtype=jnp.int32)
    hit = local[None, :] == ladder[:, None]
    source = jnp.sum(jnp.where(hit, ladder[None, :], 0), axis=1)
    return jnp.stack([source, jnp.sum(jnp.where(hit, sequence[None, :], 0), axis=1)])


def body(hidden, seq_id, dest_page, norm_gain, w_query, q_bias, w_key, w_value, v_bias, w_out):
    pages = dest_page.shape[0]
    me = lax.axis_index("tensor")
    context = lax.axis_index("context")
    heads = w_query.shape[1] // HEAD
    cuts = [(0, 3), (3, heads)]
    order = jnp.stack([me, (me + 3) % TENSOR, (me + 1) % TENSOR, (me + 2) % TENSOR]).astype(jnp.int32)
    sequence = seq_id[::PAGE]
    group = dest_page // pages
    slots = jnp.arange(pages, dtype=jnp.int32)
    page_of = jnp.sum(jnp.where(group[None, :] == slots[:, None], slots[None, :], 0), axis=1)

    paged = hidden.reshape(pages, PAGE, hidden.shape[1])
    block = jnp.split(hidden, 2)
    width = hidden.shape[1]

    def band(array, index):
        return lax.dynamic_slice_in_dim(array, order[index] * width, width, 0)

    hold = lax.optimization_barrier

    def exchange(rows):
        return lax.all_to_all(rows, DP, split_axis=0, concat_axis=0, tiled=True)

    def beside(rows):
        return lax.ppermute(rows, "context", [(0, 1)])

    shares = w_out_shares(w_out, context, lax.axis_index(("z", "xh")), 8, cuts)
    block, shares = hold((block, shares))
    left, right = ring_near(*block)
    shares = jnp.stack(shares)
    x_left, x_right = to_right(shares, X), to_left(shares, X)
    depth = (cuts[0][1] - cuts[0][0]) * HEAD // 8
    x_top, x_low = to_right(x_left[:, :depth], X), to_left(x_right[:, depth:], X)
    shares = jnp.stack([shares, x_left, x_right, jnp.concatenate([x_top, x_low], axis=1)])

    w_query, w_key, w_value, block = hold((w_query, w_key, w_value, block))
    weights = [
        jnp.concatenate([band(w, index) for w in (w_key, w_value, w_query)], axis=1)
        for index in range(TENSOR)
    ]
    gains = [band(norm_gain, index)[None, :] for index in range(TENSOR)]
    near_gains, far_gain = jnp.stack(gains[:3]), gains[3][None]
    bias = jnp.concatenate([jnp.zeros_like(v_bias), v_bias, q_bias]).astype(jnp.float32)[None, :]

    facts = jnp.stack([jnp.take(dest_page % pages, page_of), jnp.take(sequence, page_of)], axis=1)
    facts, _ = hold((facts, block))
    facts = exchange(facts)
    facts = jnp.stack([facts, beside(facts)])
    here = places(facts[0, :, 0], facts[0, :, 1])
    there = jnp.where(context > 0, places(facts[1, :, 0], facts[1, :, 1]), here)
    source = jnp.concatenate([there[0], here[0]])
    sequence = jnp.concatenate([there[1], here[1]])

    top, low, weights, near_gains, source, sequence, shares = hold(
        (left[0], right[1], weights, near_gains, source, sequence, shares)
    )
    far = ring_far(top, low)
    z_left, z_right = to_right(shares, "z"), to_left(shares, "z")
    left, right, z_left, z_right = hold((left, right, z_left, z_right))
    z_far = (to_right(z_left[:2], "z"), to_left(z_right[2:], "z"))
    carry = project_near((block, left, right), weights[:3], near_gains)
    (first, end), (start, stop) = cuts
    split = (2 + end) * HEAD
    far, z_far = hold((far, z_far))
    w_all = place_shares([shares, z_left, z_right, *z_far])
    own, queries = project_far(group, *far, weights[3], far_gain, bias, carry, split)
    own = exchange(own)
    other = beside(own[:, :, : 2 * HEAD])
    queries, own = hold((queries, own))
    queries = exchange(queries)

    second = context.astype(jnp.int32).reshape(1)
    state = attend(end - first, 2 * HEAD, source, sequence, second, own, own)
    part_a = attend(end - first, 2 * HEAD, source, sequence, second, own, own, other, state)
    own, part_a = hold((own, part_a))
    part_b = attend(stop - start, 0, source, sequence, second, queries, own, other)
    part_a, part_b = hold((exchange(part_a), part_b))
    flat_a = part_a.reshape(pages * PAGE, -1)
    left, right = to_right(flat_a), to_left(flat_a)
    flat_b = exchange(part_b).reshape(pages * PAGE, -1)
    left, right, flat_b, w_all = hold((left, right, flat_b, w_all))
    bands = [(first * HEAD // 8, end * HEAD // 8) for first, end in cuts]
    here = me.astype(jnp.int32).reshape(1)
    half = pages * PAGE // 2
    far = ring_far(left[:half], right[half:])
    steps = [(0, bands[0]), (1, bands[0]), (2, bands[0]), (0, bands[1])]
    pieces = [(flat_a,), (left,), (right,), (flat_b,)]
    total = mix_near(page_of, here, pieces, steps, w_out, w_all)
    left, right = to_right(flat_b), to_left(flat_b)
    left, right, far, total = hold((left, right, far, total))
    last = ring_far(left[:half], right[half:])
    steps = [(3, bands[0]), (1, bands[1]), (2, bands[1])]
    total = mix_near(page_of, here, [far, (left,), (right,)], steps, w_out, w_all, total, paged)
    result = mix_far(page_of, *last, bands[1], w_all, total)
    return result.reshape(hidden.shape)


def solution(mesh):
    fine = Mesh(
        mesh.devices.reshape(4, 2, 2, 2, TENSOR), ("z", "xh", "core", "context", "tensor")
    )
    rows = DP + ("context",)
    return jax.shard_map(
        body,
        mesh=fine,
        in_specs=(
            P(rows, "tensor"),
            P(rows),
            P(rows),
            P(),
            P(None, "tensor"),
            P("tensor"),
            P(None, "tensor"),
            P(None, "tensor"),
            P("tensor"),
            P("tensor", None),
        ),
        out_specs=P(rows, "tensor"),
        check_vma=False,
    )
```

```python
import math

import jax
import jax.numpy as jnp
from jax import lax
from jax.experimental import pallas as pl
from jax.experimental.pallas import tpu as pltpu
from jax.sharding import Mesh
from jax.sharding import PartitionSpec as P

HEAD = 128
PAGE = 64
EPSILON = 1e-06
DP = ("z", "xh", "core")
TENSOR = 4
RING = 4
X = ("xh", "context")
MIB = 1024 * 1024
SMALL = pl.CostEstimate(flops=1024, bytes_accessed=1024, transcendentals=0)


def to_right(block, axis="tensor"):
    return lax.ppermute(block, axis, [(i, (i + 1) % RING) for i in range(RING)])


def to_left(block, axis="tensor"):
    return lax.ppermute(block, axis, [(i, (i - 1) % RING) for i in range(RING)])


def ring_near(top, low):
    return (to_right(top), to_right(low)), (to_left(top), to_left(low))


def ring_far(left, right):
    return to_right(left), to_left(right)


def project_near_kernel(count, *refs):
    pieces, weights, gains = refs[: 2 * count], refs[2 * count : 3 * count], refs[3 * count]
    total, squares = refs[3 * count + 1 :]
    step = pl.program_id(0)
    for index in range(count):

        @pl.when(step == index)
        def _(index=index):
            for half in range(2):
                piece = pieces[2 * index + half]
                at = pl.ds(half * piece.shape[0], piece.shape[0])
                product, square = banded(piece, gains[index], weights[index])
                if index == 0:
                    total[at], squares[at] = product, square
                else:
                    total[at], squares[at] = total[at] + product, squares[at] + square


def banded(piece, gain, weights):
    wide = piece[...].astype(jnp.float32)
    scaled = (wide * gain.astype(jnp.float32)).astype(jnp.bfloat16)
    product = jnp.dot(scaled, weights[...], preferred_element_type=jnp.float32)
    return product, jnp.sum(wide * wide, axis=1, keepdims=True)


def project_near(pieces, weights, gains):
    count = len(pieces)
    half, width = pieces[0][0].shape
    rows = 2 * half
    pieces = [half for piece in pieces for half in piece]
    columns = weights[0].shape[1]
    sums = [(rows, columns), (rows, 1)]

    def kernel(*refs):
        project_near_kernel(count, *refs)

    def whole(shape):
        return pl.BlockSpec(shape, lambda k: (0,) * len(shape))

    return pl.pallas_call(
        kernel,
        out_shape=[jax.ShapeDtypeStruct(shape, jnp.float32) for shape in sums],
        grid=(count,),
        in_specs=[whole((half, width)) for _ in pieces]
        + [whole(a.shape) for a in (*weights, gains)],
        out_specs=[whole(shape) for shape in sums],
        compiler_params=pltpu.CompilerParams(vmem_limit_bytes=56 * MIB),
        cost_estimate=SMALL,
        name="project_near",
    )(*pieces, *weights, gains)


def project_far_kernel(blocks, group, top, low, weights, gain, bias, total, squares, *outs):
    step = pl.program_id(0)
    pages, count, _ = outs[0].shape
    features = TENSOR * top.shape[1]

    def finish(piece):
        product, square = banded(piece, gain[0], weights)
        scale = lax.rsqrt((squares[...] + square) * (1.0 / features) + EPSILON)
        result = ((total[...] + product) * scale + bias[...]).astype(jnp.bfloat16)
        for item in range(pages // blocks):
            target = group[step * (pages // blocks) + item]
            rows = result[item * count : (item + 1) * count]
            at = 0
            for out in outs:
                out[target] = rows[:, at : at + out.shape[2]]
                at += out.shape[2]

    pl.when(step < blocks // 2)(lambda: finish(top))
    pl.when(step >= blocks // 2)(lambda: finish(low))


def project_far(group, top, low, weights, gain, bias, carry, split):
    blocks = 4
    half, width = carry[0].shape[0] // 2, top.shape[1]
    columns = weights.shape[1]
    pages = group.shape[0]
    block = 2 * half // blocks
    shapes = [(pages, 2 * half // pages, wide) for wide in (split, columns - split)]

    def kernel(*refs):
        project_far_kernel(blocks, *refs)

    def whole(shape):
        return pl.BlockSpec(shape, lambda r, group: (0,) * len(shape))

    return pl.pallas_call(
        kernel,
        out_shape=[jax.ShapeDtypeStruct(shape, jnp.bfloat16) for shape in shapes],
        grid_spec=pltpu.PrefetchScalarGridSpec(
            num_scalar_prefetch=1,
            grid=(blocks,),
            in_specs=[
                pl.BlockSpec((block, width), lambda r, group: (jnp.minimum(r, blocks // 2 - 1), 0)),
                pl.BlockSpec((block, width), lambda r, group: (jnp.maximum(r - blocks // 2, 0), 0)),
                whole(weights.shape),
                whole(gain.shape),
                whole(bias.shape),
                pl.BlockSpec((block, columns), lambda r, group: (r, 0)),
                pl.BlockSpec((block, 1), lambda r, group: (r, 0)),
            ],
            out_specs=[whole(shape) for shape in shapes],
        ),
        compiler_params=pltpu.CompilerParams(vmem_limit_bytes=28 * MIB),
        cost_estimate=SMALL,
        name="project_far",
    )(group, top, low, weights, gain, bias, *carry)


def attend_kernel(heads, first, begins, ends, source, sequence, context, queries, own, *refs):
    refs = list(refs)
    other = refs.pop(0) if ends else None
    state_in = [] if begins else [refs.pop(0) for _ in range(3)]
    outs = [refs.pop(0) for _ in range(1 if ends else 3)]
    keys, values, turned, best, total, summed = refs
    pages = own.shape[0]
    half = pages * PAGE
    per = 4
    rows = per * PAGE
    blocks = pages // per
    lanes = heads * rows
    factor = math.log2(math.e) / math.sqrt(HEAD)

    def place_page(slot, carry):
        for base, lookup, array in [(0, 0, other)] * ends + [(half, pages, own)] * begins:
            page = source[lookup + slot]
            at = pl.ds(pl.multiple_of(base + slot * PAGE, PAGE), PAGE)
            keys[at, :] = array[page, :, :HEAD]
            values[at, :] = array[page, :, HEAD : 2 * HEAD]
        return carry

    lax.fori_loop(0, pages, place_page, 0)
    for block in range(0 if ends else blocks, 2 * blocks if begins else blocks):
        turned[block] = values[pl.ds(block * rows, rows), :].astype(jnp.float32).T.astype(jnp.bfloat16)

    def query_block(index, carry):
        slot = index * per
        query = jnp.concatenate(
            [
                queries[source[pages + slot + page], :, first + head * HEAD : first + (head + 1) * HEAD]
                for head in range(heads)
                for page in range(per)
            ],
            axis=0,
        )
        sequence_q = [sequence[pages + slot + page] for page in range(per)]
        within = lax.broadcasted_iota(jnp.int32, (1, lanes), 1) % rows
        seq_lane = jnp.full((1, lanes), sequence_q[per - 1], jnp.int32)
        for page in range(per - 2, -1, -1):
            seq_lane = jnp.where(within < (page + 1) * PAGE, sequence_q[page], seq_lane)

        def scores_of(block, diagonal):
            at = pl.ds(pl.multiple_of(block * rows, rows), rows)
            scores = lax.dot_general(
                keys[at, :], query, (((1,), (1,)), ((), ())), preferred_element_type=jnp.float32
            )
            cut = []
            for page in range(per):
                visible = seq_lane == sequence[block * per + page]
                if diagonal:
                    place = lax.broadcasted_iota(jnp.int32, (PAGE, lanes), 0) + page * PAGE
                    visible = visible & (place <= within)
                cut.append(jnp.where(visible, scores[page * PAGE : (page + 1) * PAGE], -1e30))
            return jnp.concatenate(cut, axis=0)

        def apply(block, weight):
            return jnp.dot(
                turned[block], weight.astype(jnp.bfloat16), preferred_element_type=jnp.float32
            )

        last = blocks + index
        if begins:
            scores = scores_of(last, True)
            top = jnp.max(scores, axis=0, keepdims=True)
            weight = jnp.exp2((scores - top) * factor)
            best[...] = top
            total[...] = jnp.sum(weight, axis=0, keepdims=True)
            summed[...] = apply(last, weight)
        else:
            for held, array in zip((best, total, summed), state_in):
                held[...] = array[index]

        def key_block(block, carry):
            seen = False
            for page in range(per):
                for seq in sequence_q:
                    seen = seen | (sequence[block * per + page] == seq)

            @pl.when(seen)
            def _():
                scores = scores_of(block, False)
                top = jnp.maximum(best[...], jnp.max(scores, axis=0, keepdims=True))
                weight = jnp.exp2((scores - top) * factor)
                fade = jnp.exp2((best[...] - top) * factor)
                best[...] = top
                total[...] = total[...] * fade + jnp.sum(weight, axis=0, keepdims=True)
                summed[...] = summed[...] * fade + apply(block, weight)

            return carry

        begin = jnp.where(context[0] > 0, 0, blocks) if ends else blocks
        lax.fori_loop(begin, last if begins else blocks, key_block, 0)
        if not ends:
            for held, array in zip((best, total, summed), outs):
                array[index] = held[...]
            return carry
        result = (summed[...] / total[...]).T.astype(jnp.bfloat16)
        for head in range(heads):
            for page in range(per):
                start = head * rows + page * PAGE
                outs[0][source[pages + slot + page], :, head * HEAD : (head + 1) * HEAD] = result[
                    start : start + PAGE
                ]
        return carry

    lax.fori_loop(0, blocks, query_block, 0)


def attend(heads, first, source, sequence, context, queries, own, other=None, state=None):
    pages = own.shape[0]
    begins, ends = state is None, other is not None

    def kernel(*refs):
        attend_kernel(heads, first, begins, ends, *refs)

    half = pages * PAGE
    lanes = heads * 4 * PAGE
    vmem = pl.BlockSpec(memory_space=pltpu.VMEM)
    smem = pl.BlockSpec(memory_space=pltpu.SMEM)
    operands = [queries, own] + ([other] if ends else []) + list(state or [])
    if ends:
        out_shape = [jax.ShapeDtypeStruct((pages, PAGE, heads * HEAD), jnp.bfloat16)]
    else:
        out_shape = [
            jax.ShapeDtypeStruct((pages // 4, rows, lanes), jnp.float32) for rows in (1, 1, HEAD)
        ]
    outs = pl.pallas_call(
        kernel,
        out_shape=out_shape,
        in_specs=[smem] * 3 + [vmem] * len(operands),
        out_specs=[vmem] * len(out_shape),
        scratch_shapes=[
            pltpu.VMEM((2 * half, HEAD), jnp.bfloat16),
            pltpu.VMEM((2 * half, HEAD), jnp.bfloat16),
            pltpu.VMEM((pages // 2, HEAD, 4 * PAGE), jnp.bfloat16),
            pltpu.VMEM((1, lanes), jnp.float32),
            pltpu.VMEM((1, lanes), jnp.float32),
            pltpu.VMEM((HEAD, lanes), jnp.float32),
        ],
        compiler_params=pltpu.CompilerParams(vmem_limit_bytes=20 * MIB),
        cost_estimate=SMALL,
        name="attend",
    )(source, sequence, context, *operands)
    return outs[0] if ends else outs


def rows_of(w_out, place, cut):
    begin, end = cut
    return w_out[:, 0, place, begin:end, :].reshape(-1, w_out.shape[-1])


def mix_near_kernel(steps, counts, carried, paged, page_of, me, *refs):
    refs = list(refs)
    pieces = [[refs.pop(0) for _ in range(count)] for count in counts]
    w_own, w_all = refs.pop(0), refs.pop(0)
    before = refs.pop(0) if carried else None
    hidden = refs.pop(0) if paged else None
    (total,) = refs
    block = pl.program_id(1)
    bands = [
        w_own[8 * cut[0] : 8 * cut[1], :] if place == 0 else rows_of(w_all, place - 1, cut)
        for place, cut in steps
    ]
    band = jnp.concatenate(bands, axis=0)

    def finish(half):
        rows = jnp.concatenate([piece[min(half, len(piece) - 1)][...] for piece in pieces], axis=1)
        product = jnp.dot(rows, band, preferred_element_type=jnp.float32)
        if carried:
            product = before[...] + product
        if paged:
            count = rows.shape[0] // PAGE
            added = [hidden[page_of[half * count + item]] for item in range(count)]
            product = product + jnp.concatenate(added, axis=0).astype(jnp.float32)
        total[...] = product

    for half in range(2):
        pl.when(block == half)(lambda half=half: finish(half))


def mix_near(page_of, me, pieces, steps, w_out, w_all, before=None, hidden=None):
    outer, cuts, places, stored, columns = w_all.shape
    counts = [len(piece) for piece in pieces]
    half = sum(p.shape[0] for p in pieces[0]) // 2

    def kernel(*refs):
        mix_near_kernel(steps, counts, before is not None, hidden is not None, *refs)

    flat = pl.BlockSpec((half, columns), lambda n, r, page_of, me: (r, n))
    operands, in_specs = [], []
    for piece in pieces:
        for array in piece:
            operands.append(array)
            whole = len(piece) > 1
            in_specs.append(
                pl.BlockSpec(
                    (half, array.shape[1]),
                    lambda n, r, page_of, me, whole=whole: (0 if whole else r, 0),
                )
            )
    operands += [w_out, w_all]
    in_specs += [
        pl.BlockSpec((w_out.shape[0], columns), lambda n, r, page_of, me: (0, me[0] * cuts + n)),
        pl.BlockSpec(
            (outer, 1, places, stored, columns), lambda n, r, page_of, me: (0, n, 0, 0, 0)
        ),
    ]
    if before is not None:
        operands.append(before)
        in_specs.append(flat)
    if hidden is not None:
        operands.append(hidden)
        in_specs.append(
            pl.BlockSpec((2 * half // PAGE, PAGE, columns), lambda n, r, page_of, me: (0, 0, n))
        )
    return pl.pallas_call(
        kernel,
        out_shape=jax.ShapeDtypeStruct((2 * half, cuts * columns), jnp.float32),
        grid_spec=pltpu.PrefetchScalarGridSpec(
            num_scalar_prefetch=2,
            grid=(cuts, 2),
            in_specs=in_specs,
            out_specs=flat,
        ),
        compiler_params=pltpu.CompilerParams(vmem_limit_bytes=36 * MIB),
        cost_estimate=SMALL,
        name="mix_near",
    )(page_of, me, *operands)


def mix_far_kernel(blocks, cut, page_of, top, low, w_all, before, out):
    step = pl.program_id(1)
    band = rows_of(w_all, 0, cut)

    def finish(piece):
        rows = before[...] + jnp.dot(piece[...], band, preferred_element_type=jnp.float32)
        rows = rows.astype(jnp.bfloat16)
        count = rows.shape[0] // PAGE
        for item in range(count):
            out[page_of[step * count + item]] = rows[item * PAGE : (item + 1) * PAGE]

    pl.when(step < blocks // 2)(lambda: finish(top))
    pl.when(step >= blocks // 2)(lambda: finish(low))


def mix_far(page_of, top, low, cut, w_all, before):
    blocks = 2
    half, width = top.shape
    outer, cuts, places, stored, columns = w_all.shape
    block = 2 * half // blocks
    pages = 2 * half // PAGE

    def kernel(*refs):
        mix_far_kernel(blocks, cut, *refs)

    return pl.pallas_call(
        kernel,
        out_shape=jax.ShapeDtypeStruct((pages, PAGE, cuts * columns), jnp.bfloat16),
        grid_spec=pltpu.PrefetchScalarGridSpec(
            num_scalar_prefetch=1,
            grid=(cuts, blocks),
            in_specs=[
                pl.BlockSpec((block, width), lambda n, r, page_of: (jnp.minimum(r, blocks // 2 - 1), 0)),
                pl.BlockSpec((block, width), lambda n, r, page_of: (jnp.maximum(r - blocks // 2, 0), 0)),
                pl.BlockSpec(
                    (outer, 1, 1, stored, columns), lambda n, r, page_of: (0, n, places - 1, 0, 0)
                ),
                pl.BlockSpec((block, columns), lambda n, r, page_of: (r, n)),
            ],
            out_specs=pl.BlockSpec((pages, PAGE, columns), lambda n, r, page_of: (0, 0, n)),
        ),
        compiler_params=pltpu.CompilerParams(vmem_limit_bytes=20 * MIB),
        cost_estimate=SMALL,
        name="mix_far",
    )(page_of, top, low, w_all, before)


def w_out_shares(w_out, context, outer_index, outer, cuts):
    columns = w_out.shape[1] // (2 * TENSOR)
    bands = []
    for first, end in cuts:
        depth = (end - first) * HEAD // outer
        bands.append(
            lax.dynamic_slice_in_dim(w_out, first * HEAD + outer_index * depth, depth, 0)
        )
    band = jnp.concatenate(bands, axis=0)
    me = lax.axis_index("tensor")
    right, far, left = [
        lax.dynamic_slice_in_dim(band, ((me + step) % TENSOR * 2 + context) * columns, columns, 1)
        for step in range(1, TENSOR)
    ]
    far = lax.ppermute(far, "tensor", [(i, (i + 2) % TENSOR) for i in range(TENSOR)])
    return [to_right(right), to_left(left), far]


def place_kernel(where, *refs):
    sources, out = refs[:-1], refs[-1]
    every = (0, 3, 1, 2)
    for z_step, x_steps, source in zip((*every, 2), (every, every, every, every[:2], every[2:]), sources):
        z = lax.rem(where[0] + z_step, RING)
        for index, x_step in enumerate(x_steps):
            x = lax.rem(where[1] + x_step, RING)
            out[z * 2 + x // 2, lax.rem(x, 2)] = source[index]


def place_shares(sources):
    where = jnp.stack([lax.axis_index("z"), lax.axis_index(X)]).astype(jnp.int32)
    vmem = pl.BlockSpec(memory_space=pltpu.VMEM)
    return pl.pallas_call(
        place_kernel,
        out_shape=jax.ShapeDtypeStruct((8, 2) + sources[0].shape[1:], jnp.bfloat16),
        in_specs=[pl.BlockSpec(memory_space=pltpu.SMEM)] + [vmem] * len(sources),
        out_specs=vmem,
        compiler_params=pltpu.CompilerParams(vmem_limit_bytes=60 * MIB),
        cost_estimate=SMALL,
        name="place_shares",
    )(where, *sources)


def places(local, sequence):
    pages = local.shape[0]
    ladder = jnp.arange(pages, dtype=jnp.int32)
    hit = local[None, :] == ladder[:, None]
    source = jnp.sum(jnp.where(hit, ladder[None, :], 0), axis=1)
    return jnp.stack([source, jnp.sum(jnp.where(hit, sequence[None, :], 0), axis=1)])


def body(hidden, seq_id, dest_page, norm_gain, w_query, q_bias, w_key, w_value, v_bias, w_out):
    pages = dest_page.shape[0]
    me = lax.axis_index("tensor")
    context = lax.axis_index("context")
    heads = w_query.shape[1] // HEAD
    cuts = [(0, 3), (3, heads)]
    order = jnp.stack([me, (me + 3) % TENSOR, (me + 1) % TENSOR, (me + 2) % TENSOR]).astype(jnp.int32)
    sequence = seq_id[::PAGE]
    group = dest_page // pages
    slots = jnp.arange(pages, dtype=jnp.int32)
    page_of = jnp.sum(jnp.where(group[None, :] == slots[:, None], slots[None, :], 0), axis=1)

    paged = hidden.reshape(pages, PAGE, hidden.shape[1])
    block = jnp.split(hidden, 2)
    width = hidden.shape[1]

    def band(array, index):
        return lax.dynamic_slice_in_dim(array, order[index] * width, width, 0)

    hold = lax.optimization_barrier

    def exchange(rows):
        return lax.all_to_all(rows, DP, split_axis=0, concat_axis=0, tiled=True)

    def beside(rows):
        return lax.ppermute(rows, "context", [(0, 1)])

    shares = w_out_shares(w_out, context, lax.axis_index(("z", "xh")), 8, cuts)
    block, shares = hold((block, shares))
    left, right = ring_near(*block)
    shares = jnp.stack(shares)
    x_left, x_right = to_right(shares, X), to_left(shares, X)
    depth = (cuts[0][1] - cuts[0][0]) * HEAD // 8
    x_top, x_low = to_right(x_left[:, :depth], X), to_left(x_right[:, depth:], X)
    shares = jnp.stack([shares, x_left, x_right, jnp.concatenate([x_top, x_low], axis=1)])

    w_query, w_key, w_value, block = hold((w_query, w_key, w_value, block))
    weights = [
        jnp.concatenate([band(w, index) for w in (w_key, w_value, w_query)], axis=1)
        for index in range(TENSOR)
    ]
    gains = [band(norm_gain, index)[None, :] for index in range(TENSOR)]
    near_gains, far_gain = jnp.stack(gains[:3]), gains[3][None]
    bias = jnp.concatenate([jnp.zeros_like(v_bias), v_bias, q_bias]).astype(jnp.float32)[None, :]

    facts = jnp.stack([jnp.take(dest_page % pages, page_of), jnp.take(sequence, page_of)], axis=1)
    facts, _ = hold((facts, block))
    facts = exchange(facts)
    facts = jnp.stack([facts, beside(facts)])
    here = places(facts[0, :, 0], facts[0, :, 1])
    there = jnp.where(context > 0, places(facts[1, :, 0], facts[1, :, 1]), here)
    source = jnp.concatenate([there[0], here[0]])
    sequence = jnp.concatenate([there[1], here[1]])

    top, low, weights, near_gains, source, sequence, shares = hold(
        (left[0], right[1], weights, near_gains, source, sequence, shares)
    )
    far = ring_far(top, low)
    z_left, z_right = to_right(shares, "z"), to_left(shares, "z")
    left, right, z_left, z_right = hold((left, right, z_left, z_right))
    z_far = (to_right(z_left[:2], "z"), to_left(z_right[2:], "z"))
    carry = project_near((block, left, right), weights[:3], near_gains)
    (first, end), (start, stop) = cuts
    split = (2 + end) * HEAD
    far, z_far = hold((far, z_far))
    w_all = place_shares([shares, z_left, z_right, *z_far])
    own, queries = project_far(group, *far, weights[3], far_gain, bias, carry, split)
    own = exchange(own)
    other = beside(own[:, :, : 2 * HEAD])
    queries, own = hold((queries, own))
    queries = exchange(queries)

    second = context.astype(jnp.int32).reshape(1)
    state = attend(end - first, 2 * HEAD, source, sequence, second, own, own)
    part_a = attend(end - first, 2 * HEAD, source, sequence, second, own, own, other, state)
    own, part_a = hold((own, part_a))
    part_b = attend(stop - start, 0, source, sequence, second, queries, own, other)
    part_a, part_b = hold((exchange(part_a), part_b))
    flat_a = part_a.reshape(pages * PAGE, -1)
    left, right = to_right(flat_a), to_left(flat_a)
    flat_b = exchange(part_b).reshape(pages * PAGE, -1)
    left, right, flat_b, w_all = hold((left, right, flat_b, w_all))
    bands = [(first * HEAD // 8, end * HEAD // 8) for first, end in cuts]
    here = me.astype(jnp.int32).reshape(1)
    half = pages * PAGE // 2
    far = ring_far(left[:half], right[half:])
    steps = [(0, bands[0]), (1, bands[0]), (2, bands[0]), (0, bands[1])]
    pieces = [(flat_a,), (left,), (right,), (flat_b,)]
    total = mix_near(page_of, here, pieces, steps, w_out, w_all)
    left, right = to_right(flat_b), to_left(flat_b)
    left, right, far, total = hold((left, right, far, total))
    last = ring_far(left[:half], right[half:])
    steps = [(3, bands[0]), (1, bands[1]), (2, bands[1])]
    total = mix_near(page_of, here, [far, (left,), (right,)], steps, w_out, w_all, total, paged)
    result = mix_far(page_of, *last, bands[1], w_all, total)
    return result.reshape(hidden.shape)


def solution(mesh):
    fine = Mesh(
        mesh.devices.reshape(4, 2, 2, 2, TENSOR), ("z", "xh", "core", "context", "tensor")
    )
    rows = DP + ("context",)
    return jax.shard_map(
        body,
        mesh=fine,
        in_specs=(
            P(rows, "tensor"),
            P(rows),
            P(rows),
            P(),
            P(None, "tensor"),
            P("tensor"),
            P(None, "tensor"),
            P(None, "tensor"),
            P("tensor"),
            P("tensor", None),
        ),
        out_specs=P(rows, "tensor"),
        check_vma=False,
    )
```

```python
import math

import jax
import jax.numpy as jnp
from jax import lax
from jax.experimental import pallas as pl
from jax.experimental.pallas import tpu as pltpu
from jax.sharding import Mesh
from jax.sharding import PartitionSpec as P

HEAD = 128
PAGE = 64
EPSILON = 1e-06
DP = ("z", "xh", "core")
TENSOR = 4
RING = 4
X = ("xh", "context")
MIB = 1024 * 1024
SMALL = pl.CostEstimate(flops=1024, bytes_accessed=1024, transcendentals=0)


def to_right(block, axis="tensor"):
    return lax.ppermute(block, axis, [(i, (i + 1) % RING) for i in range(RING)])


def to_left(block, axis="tensor"):
    return lax.ppermute(block, axis, [(i, (i - 1) % RING) for i in range(RING)])


def ring_near(top, low):
    return (to_right(top), to_right(low)), (to_left(top), to_left(low))


def ring_far(left, right):
    return to_right(left), to_left(right)


def project_near_kernel(count, *refs):
    pieces, weights, gains = refs[: 2 * count], refs[2 * count : 3 * count], refs[3 * count]
    total, squares = refs[3 * count + 1 :]
    step = pl.program_id(0)
    for index in range(count):

        @pl.when(step == index)
        def _(index=index):
            for half in range(2):
                piece = pieces[2 * index + half]
                at = pl.ds(half * piece.shape[0], piece.shape[0])
                product, square = banded(piece, gains[index], weights[index])
                if index == 0:
                    total[at], squares[at] = product, square
                else:
                    total[at], squares[at] = total[at] + product, squares[at] + square


def banded(piece, gain, weights):
    wide = piece[...].astype(jnp.float32)
    scaled = (wide * gain.astype(jnp.float32)).astype(jnp.bfloat16)
    product = jnp.dot(scaled, weights[...], preferred_element_type=jnp.float32)
    return product, jnp.sum(wide * wide, axis=1, keepdims=True)


def project_near(pieces, weights, gains):
    count = len(pieces)
    half, width = pieces[0][0].shape
    rows = 2 * half
    pieces = [half for piece in pieces for half in piece]
    columns = weights[0].shape[1]
    sums = [(rows, columns), (rows, 1)]

    def kernel(*refs):
        project_near_kernel(count, *refs)

    def whole(shape):
        return pl.BlockSpec(shape, lambda k: (0,) * len(shape))

    return pl.pallas_call(
        kernel,
        out_shape=[jax.ShapeDtypeStruct(shape, jnp.float32) for shape in sums],
        grid=(count,),
        in_specs=[whole((half, width)) for _ in pieces]
        + [whole(a.shape) for a in (*weights, gains)],
        out_specs=[whole(shape) for shape in sums],
        compiler_params=pltpu.CompilerParams(vmem_limit_bytes=56 * MIB),
        cost_estimate=SMALL,
        name="project_near",
    )(*pieces, *weights, gains)


def project_far_kernel(blocks, group, top, low, weights, gain, bias, total, squares, *outs):
    step = pl.program_id(0)
    pages, count, _ = outs[0].shape
    features = TENSOR * top.shape[1]

    def finish(piece):
        product, square = banded(piece, gain[0], weights)
        scale = lax.rsqrt((squares[...] + square) * (1.0 / features) + EPSILON)
        result = ((total[...] + product) * scale + bias[...]).astype(jnp.bfloat16)
        for item in range(pages // blocks):
            target = group[step * (pages // blocks) + item]
            rows = result[item * count : (item + 1) * count]
            at = 0
            for out in outs:
                out[target] = rows[:, at : at + out.shape[2]]
                at += out.shape[2]

    pl.when(step < blocks // 2)(lambda: finish(top))
    pl.when(step >= blocks // 2)(lambda: finish(low))


def project_far(group, top, low, weights, gain, bias, carry, split):
    blocks = 4
    half, width = carry[0].shape[0] // 2, top.shape[1]
    columns = weights.shape[1]
    pages = group.shape[0]
    block = 2 * half // blocks
    shapes = [(pages, 2 * half // pages, wide) for wide in (split, columns - split)]

    def kernel(*refs):
        project_far_kernel(blocks, *refs)

    def whole(shape):
        return pl.BlockSpec(shape, lambda r, group: (0,) * len(shape))

    return pl.pallas_call(
        kernel,
        out_shape=[jax.ShapeDtypeStruct(shape, jnp.bfloat16) for shape in shapes],
        grid_spec=pltpu.PrefetchScalarGridSpec(
            num_scalar_prefetch=1,
            grid=(blocks,),
            in_specs=[
                pl.BlockSpec((block, width), lambda r, group: (jnp.minimum(r, blocks // 2 - 1), 0)),
                pl.BlockSpec((block, width), lambda r, group: (jnp.maximum(r - blocks // 2, 0), 0)),
                whole(weights.shape),
                whole(gain.shape),
                whole(bias.shape),
                pl.BlockSpec((block, columns), lambda r, group: (r, 0)),
                pl.BlockSpec((block, 1), lambda r, group: (r, 0)),
            ],
            out_specs=[whole(shape) for shape in shapes],
        ),
        compiler_params=pltpu.CompilerParams(vmem_limit_bytes=28 * MIB),
        cost_estimate=SMALL,
        name="project_far",
    )(group, top, low, weights, gain, bias, *carry)


def attend_kernel(heads, first, begins, ends, source, sequence, context, queries, own, *refs):
    refs = list(refs)
    other = refs.pop(0) if ends else None
    state_in = [] if begins else [refs.pop(0) for _ in range(3)]
    outs = [refs.pop(0) for _ in range(1 if ends else 3)]
    keys, values, turned, best, total, summed = refs
    pages = own.shape[0]
    half = pages * PAGE
    per = 4
    rows = per * PAGE
    blocks = pages // per
    lanes = heads * rows
    factor = math.log2(math.e) / math.sqrt(HEAD)

    def place_page(slot, carry):
        for base, lookup, array in [(0, 0, other)] * ends + [(half, pages, own)] * begins:
            page = source[lookup + slot]
            at = pl.ds(pl.multiple_of(base + slot * PAGE, PAGE), PAGE)
            keys[at, :] = array[page, :, :HEAD]
            values[at, :] = array[page, :, HEAD : 2 * HEAD]
        return carry

    lax.fori_loop(0, pages, place_page, 0)
    for block in range(0 if ends else blocks, 2 * blocks if begins else blocks):
        turned[block] = values[pl.ds(block * rows, rows), :].astype(jnp.float32).T.astype(jnp.bfloat16)

    def query_block(index, carry):
        slot = index * per
        query = jnp.concatenate(
            [
                queries[source[pages + slot + page], :, first + head * HEAD : first + (head + 1) * HEAD]
                for head in range(heads)
                for page in range(per)
            ],
            axis=0,
        )
        sequence_q = [sequence[pages + slot + page] for page in range(per)]
        within = lax.broadcasted_iota(jnp.int32, (1, lanes), 1) % rows
        seq_lane = jnp.full((1, lanes), sequence_q[per - 1], jnp.int32)
        for page in range(per - 2, -1, -1):
            seq_lane = jnp.where(within < (page + 1) * PAGE, sequence_q[page], seq_lane)

        def scores_of(block, diagonal):
            at = pl.ds(pl.multiple_of(block * rows, rows), rows)
            scores = lax.dot_general(
                keys[at, :], query, (((1,), (1,)), ((), ())), preferred_element_type=jnp.float32
            )
            cut = []
            for page in range(per):
                visible = seq_lane == sequence[block * per + page]
                if diagonal:
                    place = lax.broadcasted_iota(jnp.int32, (PAGE, lanes), 0) + page * PAGE
                    visible = visible & (place <= within)
                cut.append(jnp.where(visible, scores[page * PAGE : (page + 1) * PAGE], -1e30))
            return jnp.concatenate(cut, axis=0)

        def apply(block, weight):
            return jnp.dot(
                turned[block], weight.astype(jnp.bfloat16), preferred_element_type=jnp.float32
            )

        last = blocks + index
        if begins:
            scores = scores_of(last, True)
            top = jnp.max(scores, axis=0, keepdims=True)
            weight = jnp.exp2((scores - top) * factor)
            best[...] = top
            total[...] = jnp.sum(weight, axis=0, keepdims=True)
            summed[...] = apply(last, weight)
        else:
            for held, array in zip((best, total, summed), state_in):
                held[...] = array[index]

        def key_block(block, carry):
            seen = False
            for page in range(per):
                for seq in sequence_q:
                    seen = seen | (sequence[block * per + page] == seq)

            @pl.when(seen)
            def _():
                scores = scores_of(block, False)
                top = jnp.maximum(best[...], jnp.max(scores, axis=0, keepdims=True))
                weight = jnp.exp2((scores - top) * factor)
                fade = jnp.exp2((best[...] - top) * factor)
                best[...] = top
                total[...] = total[...] * fade + jnp.sum(weight, axis=0, keepdims=True)
                summed[...] = summed[...] * fade + apply(block, weight)

            return carry

        begin = jnp.where(context[0] > 0, 0, blocks) if ends else blocks
        lax.fori_loop(begin, last if begins else blocks, key_block, 0)
        if not ends:
            for held, array in zip((best, total, summed), outs):
                array[index] = held[...]
            return carry
        result = (summed[...] / total[...]).T.astype(jnp.bfloat16)
        for head in range(heads):
            for page in range(per):
                start = head * rows + page * PAGE
                outs[0][source[pages + slot + page], :, head * HEAD : (head + 1) * HEAD] = result[
                    start : start + PAGE
                ]
        return carry

    lax.fori_loop(0, blocks, query_block, 0)


def attend(heads, first, source, sequence, context, queries, own, other=None, state=None):
    pages = own.shape[0]
    begins, ends = state is None, other is not None

    def kernel(*refs):
        attend_kernel(heads, first, begins, ends, *refs)

    half = pages * PAGE
    lanes = heads * 4 * PAGE
    vmem = pl.BlockSpec(memory_space=pltpu.VMEM)
    smem = pl.BlockSpec(memory_space=pltpu.SMEM)
    operands = [queries, own] + ([other] if ends else []) + list(state or [])
    if ends:
        out_shape = [jax.ShapeDtypeStruct((pages, PAGE, heads * HEAD), jnp.bfloat16)]
    else:
        out_shape = [
            jax.ShapeDtypeStruct((pages // 4, rows, lanes), jnp.float32) for rows in (1, 1, HEAD)
        ]
    outs = pl.pallas_call(
        kernel,
        out_shape=out_shape,
        in_specs=[smem] * 3 + [vmem] * len(operands),
        out_specs=[vmem] * len(out_shape),
        scratch_shapes=[
            pltpu.VMEM((2 * half, HEAD), jnp.bfloat16),
            pltpu.VMEM((2 * half, HEAD), jnp.bfloat16),
            pltpu.VMEM((pages // 2, HEAD, 4 * PAGE), jnp.bfloat16),
            pltpu.VMEM((1, lanes), jnp.float32),
            pltpu.VMEM((1, lanes), jnp.float32),
            pltpu.VMEM((HEAD, lanes), jnp.float32),
        ],
        compiler_params=pltpu.CompilerParams(vmem_limit_bytes=20 * MIB),
        cost_estimate=SMALL,
        name="attend",
    )(source, sequence, context, *operands)
    return outs[0] if ends else outs


def rows_of(w_out, place, cut):
    begin, end = cut
    return w_out[:, 0, place, begin:end, :].reshape(-1, w_out.shape[-1])


def mix_near_kernel(steps, counts, carried, paged, page_of, me, *refs):
    refs = list(refs)
    pieces = [[refs.pop(0) for _ in range(count)] for count in counts]
    w_own, w_all = refs.pop(0), refs.pop(0)
    before = refs.pop(0) if carried else None
    hidden = refs.pop(0) if paged else None
    (total,) = refs
    block = pl.program_id(1)
    bands = [
        w_own[8 * cut[0] : 8 * cut[1], :] if place == 0 else rows_of(w_all, place - 1, cut)
        for place, cut in steps
    ]
    band = jnp.concatenate(bands, axis=0)

    def finish(half):
        rows = jnp.concatenate([piece[min(half, len(piece) - 1)][...] for piece in pieces], axis=1)
        product = jnp.dot(rows, band, preferred_element_type=jnp.float32)
        if carried:
            product = before[...] + product
        if paged:
            count = rows.shape[0] // PAGE
            added = [hidden[page_of[half * count + item]] for item in range(count)]
            product = product + jnp.concatenate(added, axis=0).astype(jnp.float32)
        total[...] = product

    for half in range(2):
        pl.when(block == half)(lambda half=half: finish(half))


def mix_near(page_of, me, pieces, steps, w_out, w_all, before=None, hidden=None):
    outer, cuts, places, stored, columns = w_all.shape
    counts = [len(piece) for piece in pieces]
    half = sum(p.shape[0] for p in pieces[0]) // 2

    def kernel(*refs):
        mix_near_kernel(steps, counts, before is not None, hidden is not None, *refs)

    flat = pl.BlockSpec((half, columns), lambda n, r, page_of, me: (r, n))
    operands, in_specs = [], []
    for piece in pieces:
        for array in piece:
            operands.append(array)
            whole = len(piece) > 1
            in_specs.append(
                pl.BlockSpec(
                    (half, array.shape[1]),
                    lambda n, r, page_of, me, whole=whole: (0 if whole else r, 0),
                )
            )
    operands += [w_out, w_all]
    in_specs += [
        pl.BlockSpec((w_out.shape[0], columns), lambda n, r, page_of, me: (0, me[0] * cuts + n)),
        pl.BlockSpec(
            (outer, 1, places, stored, columns), lambda n, r, page_of, me: (0, n, 0, 0, 0)
        ),
    ]
    if before is not None:
        operands.append(before)
        in_specs.append(flat)
    if hidden is not None:
        operands.append(hidden)
        in_specs.append(
            pl.BlockSpec((2 * half // PAGE, PAGE, columns), lambda n, r, page_of, me: (0, 0, n))
        )
    return pl.pallas_call(
        kernel,
        out_shape=jax.ShapeDtypeStruct((2 * half, cuts * columns), jnp.float32),
        grid_spec=pltpu.PrefetchScalarGridSpec(
            num_scalar_prefetch=2,
            grid=(cuts, 2),
            in_specs=in_specs,
            out_specs=flat,
        ),
        compiler_params=pltpu.CompilerParams(vmem_limit_bytes=36 * MIB),
        cost_estimate=SMALL,
        name="mix_near",
    )(page_of, me, *operands)


def mix_far_kernel(blocks, cut, page_of, top, low, w_all, before, out):
    step = pl.program_id(1)
    band = rows_of(w_all, 0, cut)

    def finish(piece):
        rows = before[...] + jnp.dot(piece[...], band, preferred_element_type=jnp.float32)
        rows = rows.astype(jnp.bfloat16)
        count = rows.shape[0] // PAGE
        for item in range(count):
            out[page_of[step * count + item]] = rows[item * PAGE : (item + 1) * PAGE]

    pl.when(step < blocks // 2)(lambda: finish(top))
    pl.when(step >= blocks // 2)(lambda: finish(low))


def mix_far(page_of, top, low, cut, w_all, before):
    blocks = 2
    half, width = top.shape
    outer, cuts, places, stored, columns = w_all.shape
    block = 2 * half // blocks
    pages = 2 * half // PAGE

    def kernel(*refs):
        mix_far_kernel(blocks, cut, *refs)

    return pl.pallas_call(
        kernel,
        out_shape=jax.ShapeDtypeStruct((pages, PAGE, cuts * columns), jnp.bfloat16),
        grid_spec=pltpu.PrefetchScalarGridSpec(
            num_scalar_prefetch=1,
            grid=(cuts, blocks),
            in_specs=[
                pl.BlockSpec((block, width), lambda n, r, page_of: (jnp.minimum(r, blocks // 2 - 1), 0)),
                pl.BlockSpec((block, width), lambda n, r, page_of: (jnp.maximum(r - blocks // 2, 0), 0)),
                pl.BlockSpec(
                    (outer, 1, 1, stored, columns), lambda n, r, page_of: (0, n, places - 1, 0, 0)
                ),
                pl.BlockSpec((block, columns), lambda n, r, page_of: (r, n)),
            ],
            out_specs=pl.BlockSpec((pages, PAGE, columns), lambda n, r, page_of: (0, 0, n)),
        ),
        compiler_params=pltpu.CompilerParams(vmem_limit_bytes=20 * MIB),
        cost_estimate=SMALL,
        name="mix_far",
    )(page_of, top, low, w_all, before)


def w_out_shares(w_out, context, outer_index, outer, cuts):
    columns = w_out.shape[1] // (2 * TENSOR)
    bands = []
    for first, end in cuts:
        depth = (end - first) * HEAD // outer
        bands.append(
            lax.dynamic_slice_in_dim(w_out, first * HEAD + outer_index * depth, depth, 0)
        )
    band = jnp.concatenate(bands, axis=0)
    me = lax.axis_index("tensor")
    right, far, left = [
        lax.dynamic_slice_in_dim(band, ((me + step) % TENSOR * 2 + context) * columns, columns, 1)
        for step in range(1, TENSOR)
    ]
    far = lax.ppermute(far, "tensor", [(i, (i + 2) % TENSOR) for i in range(TENSOR)])
    return [to_right(right), to_left(left), far]


def place_kernel(where, *refs):
    sources, out = refs[:-1], refs[-1]
    every = (0, 3, 1, 2)
    for z_step, x_steps, source in zip((*every, 2), (every, every, every, every[:2], every[2:]), sources):
        z = lax.rem(where[0] + z_step, RING)
        for index, x_step in enumerate(x_steps):
            x = lax.rem(where[1] + x_step, RING)
            out[z * 2 + x // 2, lax.rem(x, 2)] = source[index]


def place_shares(sources):
    where = jnp.stack([lax.axis_index("z"), lax.axis_index(X)]).astype(jnp.int32)
    vmem = pl.BlockSpec(memory_space=pltpu.VMEM)
    return pl.pallas_call(
        place_kernel,
        out_shape=jax.ShapeDtypeStruct((8, 2) + sources[0].shape[1:], jnp.bfloat16),
        in_specs=[pl.BlockSpec(memory_space=pltpu.SMEM)] + [vmem] * len(sources),
        out_specs=vmem,
        compiler_params=pltpu.CompilerParams(vmem_limit_bytes=60 * MIB),
        cost_estimate=SMALL,
        name="place_shares",
    )(where, *sources)


def places(local, sequence):
    pages = local.shape[0]
    ladder = jnp.arange(pages, dtype=jnp.int32)
    hit = local[None, :] == ladder[:, None]
    source = jnp.sum(jnp.where(hit, ladder[None, :], 0), axis=1)
    return jnp.stack([source, jnp.sum(jnp.where(hit, sequence[None, :], 0), axis=1)])


def body(hidden, seq_id, dest_page, norm_gain, w_query, q_bias, w_key, w_value, v_bias, w_out):
    pages = dest_page.shape[0]
    me = lax.axis_index("tensor")
    context = lax.axis_index("context")
    heads = w_query.shape[1] // HEAD
    cuts = [(0, 3), (3, heads)]
    order = jnp.stack([me, (me + 3) % TENSOR, (me + 1) % TENSOR, (me + 2) % TENSOR]).astype(jnp.int32)
    sequence = seq_id[::PAGE]
    group = dest_page // pages
    slots = jnp.arange(pages, dtype=jnp.int32)
    page_of = jnp.sum(jnp.where(group[None, :] == slots[:, None], slots[None, :], 0), axis=1)

    paged = hidden.reshape(pages, PAGE, hidden.shape[1])
    block = jnp.split(hidden, 2)
    width = hidden.shape[1]

    def band(array, index):
        return lax.dynamic_slice_in_dim(array, order[index] * width, width, 0)

    hold = lax.optimization_barrier

    def exchange(rows):
        return lax.all_to_all(rows, DP, split_axis=0, concat_axis=0, tiled=True)

    def beside(rows):
        return lax.ppermute(rows, "context", [(0, 1)])

    shares = w_out_shares(w_out, context, lax.axis_index(("z", "xh")), 8, cuts)
    block, shares = hold((block, shares))
    left, right = ring_near(*block)
    shares = jnp.stack(shares)
    x_left, x_right = to_right(shares, X), to_left(shares, X)
    depth = (cuts[0][1] - cuts[0][0]) * HEAD // 8
    x_top, x_low = to_right(x_left[:, :depth], X), to_left(x_right[:, depth:], X)
    shares = jnp.stack([shares, x_left, x_right, jnp.concatenate([x_top, x_low], axis=1)])

    w_query, w_key, w_value, block = hold((w_query, w_key, w_value, block))
    weights = [
        jnp.concatenate([band(w, index) for w in (w_key, w_value, w_query)], axis=1)
        for index in range(TENSOR)
    ]
    gains = [band(norm_gain, index)[None, :] for index in range(TENSOR)]
    near_gains, far_gain = jnp.stack(gains[:3]), gains[3][None]
    bias = jnp.concatenate([jnp.zeros_like(v_bias), v_bias, q_bias]).astype(jnp.float32)[None, :]

    facts = jnp.stack([jnp.take(dest_page % pages, page_of), jnp.take(sequence, page_of)], axis=1)
    facts, _ = hold((facts, block))
    facts = exchange(facts)
    facts = jnp.stack([facts, beside(facts)])
    here = places(facts[0, :, 0], facts[0, :, 1])
    there = jnp.where(context > 0, places(facts[1, :, 0], facts[1, :, 1]), here)
    source = jnp.concatenate([there[0], here[0]])
    sequence = jnp.concatenate([there[1], here[1]])

    top, low, weights, near_gains, source, sequence, shares = hold(
        (left[0], right[1], weights, near_gains, source, sequence, shares)
    )
    far = ring_far(top, low)
    z_left, z_right = to_right(shares, "z"), to_left(shares, "z")
    left, right, z_left, z_right = hold((left, right, z_left, z_right))
    z_far = (to_right(z_left[:2], "z"), to_left(z_right[2:], "z"))
    carry = project_near((block, left, right), weights[:3], near_gains)
    (first, end), (start, stop) = cuts
    split = (2 + end) * HEAD
    far, z_far = hold((far, z_far))
    w_all = place_shares([shares, z_left, z_right, *z_far])
    own, queries = project_far(group, *far, weights[3], far_gain, bias, carry, split)
    own = exchange(own)
    other = beside(own[:, :, : 2 * HEAD])
    queries, own = hold((queries, own))
    queries = exchange(queries)

    second = context.astype(jnp.int32).reshape(1)
    state = attend(end - first, 2 * HEAD, source, sequence, second, own, own)
    part_a = attend(end - first, 2 * HEAD, source, sequence, second, own, own, other, state)
    own, part_a = hold((own, part_a))
    part_b = attend(stop - start, 0, source, sequence, second, queries, own, other)
    part_a, part_b = hold((exchange(part_a), part_b))
    flat_a = part_a.reshape(pages * PAGE, -1)
    left, right = to_right(flat_a), to_left(flat_a)
    flat_b = exchange(part_b).reshape(pages * PAGE, -1)
    left, right, flat_b, w_all = hold((left, right, flat_b, w_all))
    bands = [(first * HEAD // 8, end * HEAD // 8) for first, end in cuts]
    here = me.astype(jnp.int32).reshape(1)
    half = pages * PAGE // 2
    far = ring_far(left[:half], right[half:])
    steps = [(0, bands[0]), (1, bands[0]), (2, bands[0]), (0, bands[1])]
    pieces = [(flat_a,), (left,), (right,), (flat_b,)]
    total = mix_near(page_of, here, pieces, steps, w_out, w_all, None, paged)
    left, right = to_right(flat_b), to_left(flat_b)
    left, right, far, total = hold((left, right, far, total))
    last = ring_far(left[:half], right[half:])
    steps = [(3, bands[0]), (1, bands[1]), (2, bands[1])]
    total = mix_near(page_of, here, [far, (left,), (right,)], steps, w_out, w_all, total)
    result = mix_far(page_of, *last, bands[1], w_all, total)
    return result.reshape(hidden.shape)


def solution(mesh):
    fine = Mesh(
        mesh.devices.reshape(4, 2, 2, 2, TENSOR), ("z", "xh", "core", "context", "tensor")
    )
    rows = DP + ("context",)
    return jax.shard_map(
        body,
        mesh=fine,
        in_specs=(
            P(rows, "tensor"),
            P(rows),
            P(rows),
            P(),
            P(None, "tensor"),
            P("tensor"),
            P(None, "tensor"),
            P(None, "tensor"),
            P("tensor"),
            P("tensor", None),
        ),
        out_specs=P(rows, "tensor"),
        check_vma=False,
    )
```
